256 devices in a mesh: slab: 8 (over y, core), seq: 32 (over z, x).
Axes of the slice: x: 4, y: 4, z: 8, core: 2. Of those that a mesh axis runs over, the one named last changes fastest.
Arguments:
- noise: float32 [2, 16, 2048], P(None, None, 'seq'), may hold values from -6 to 6
- plan: int32 [32], replicated, may hold values from 1 to 1000, as said below
- slides: int32 [2], replicated, may hold values from 7 to 9
- w_in: bfloat16 [16, 1152], replicated, may hold values from -1.5 to 1.5
- w_mod: bfloat16 [256, 2304], replicated, may hold values from -0.375 to 0.375
- w_qkv: bfloat16 [1152, 3456], replicated, may hold values from -0.088388348 to 0.088388348
- qk_gain: float32 [2, 1152], replicated, may hold values from 0.5 to 6
- w_o: bfloat16 [1152, 1152], replicated, may hold values from -0.1875 to 0.1875
- w_out: bfloat16 [1152, 16], replicated, may hold values from -0.1875 to 0.1875
Outputs:
- trajectory: float32 [16, 2, 16, 2048], P('slab', None, None, 'seq')
- anchor: float32 [2, 16, 2048], P(None, None, 'seq')
The draws below stay inside these ranges and needn't reach their ends.
Inputs may be any that keep to these rules, and one draw needn't show every extreme that they name: `plan`: strictly decreasing; the first entry is 1000.
All inputs are finite; a program needn't handle non-finite values.
Results may differ from the reference program's by a relative error of at most 0.0028.
Values may be sent and summed in bfloat16 or wider, within the bound.
A program may use at most 128 MiB of HBM per device.

```python
import math
import jax
import jax.numpy as jnp
from jax import lax

D = 1152
HEADS = 16
HD = 72
PATCH = 16
FREQ = 256
CLIPS = 2
STEPS_DEV = 2
SWEEPS = 2
WINDOW = 16
TOKENS = 2048
SCHED = 32
N_SLAB = 8


def draw_plan(key, part):
    key = jax.random.fold_in(key, 5)
    picked = jax.random.permutation(key, 999)[:SCHED - 1] + 1
    falling = -jnp.sort(-picked)
    return jnp.concatenate([jnp.full((1,), 1000, jnp.int32), falling.astype(jnp.int32)])


def draw_w_qkv(key, part):
    key = jax.random.fold_in(key, 3)
    model_width = HEADS * HD
    limit = 3.0 / model_width ** 0.5
    base = jax.random.normal(key, (model_width, 3 * model_width), jnp.float32) / model_width ** 0.5
    base = jnp.clip(base, -limit, limit)
    return base.astype(jnp.bfloat16)


def draw_qk_gain(key, part):
    key = jax.random.fold_in(key, 4)
    model_width = HEADS * HD
    return jax.random.uniform(key, (2, model_width), jnp.float32, 0.5, 1.5)


def block_levels(stream_key, extent, pieces, low, top_value):
    factor_of, own = 1.0, jax.random.fold_in(stream_key, 6)
    for dim, blocks in pieces:
        draws = jnp.exp(jax.random.uniform(jax.random.fold_in(own, dim), (blocks,), jnp.float32, low / len(pieces), top_value / len(pieces)))
        factor_of = factor_of * jnp.repeat(draws, extent[dim] // blocks).reshape([-1 if axis == dim else 1 for axis in range(len(extent))])
    return factor_of


def normal_values(own_key, shape, scale, reach, pieces=(), kind=jnp.bfloat16):
    loudness = block_levels(own_key, shape, pieces, -0.22, 0.18) if pieces else 1.0
    result = jax.random.normal(own_key, shape, jnp.float32) * scale * loudness
    return jnp.minimum(jnp.maximum(result, -reach), reach).astype(kind)


def setup_inputs(seed: int = 0) -> dict:
    seeds = jax.random.split(jax.random.key(seed), 10)
    noise = normal_values(seeds[0], (CLIPS, PATCH, TOKENS), 1.0, 6.0, ((2, 32),), jnp.float32)
    plan = draw_plan(jax.random.fold_in(seeds[9], 71), 0)
    slides = jax.random.randint(seeds[2], (SWEEPS,), WINDOW // 2 - 1, WINDOW // 2 + 2).astype(jnp.int32)
    w_in = normal_values(seeds[3], (PATCH, D), PATCH ** -0.5, 1.5)
    w_mod = normal_values(seeds[4], (FREQ, 2 * D), FREQ ** -0.5, 0.375)
    w_qkv = draw_w_qkv(jax.random.fold_in(seeds[9], 71), 0)
    qk_gain = draw_qk_gain(jax.random.fold_in(seeds[9], 71), 0)
    w_o = normal_values(seeds[7], (D, D), D ** -0.5, 0.1875)
    w_out = normal_values(seeds[8], (D, PATCH), D ** -0.5, 0.1875)
    return dict(noise=noise, plan=plan, slides=slides, w_in=w_in, w_mod=w_mod, w_qkv=w_qkv, qk_gain=qk_gain, w_o=w_o, w_out=w_out)


norm_eps = 1e-06

def rounded(tensor):
    return lax.optimization_barrier(tensor.astype(jnp.bfloat16)).astype(jnp.float32)

def layer_norm(tensor):
    average = lax.optimization_barrier(jnp.mean(tensor, axis=-1, keepdims=True))
    centered = tensor - average
    spread = lax.optimization_barrier(jnp.mean(centered * centered, axis=-1, keepdims=True))
    return centered * lax.rsqrt(spread + norm_eps)

def time_features(levels, feature_count):
    half_width = feature_count // 2
    frequency = jnp.exp(-math.log(10000.0) * jnp.arange(half_width, dtype=jnp.float32) / half_width)
    angles = levels[:, None] * frequency[None, :]
    return jnp.concatenate([jnp.cos(angles), jnp.sin(angles)], axis=-1)

def head_norm(tensor, gain_row):
    inv_rms = lax.rsqrt(lax.optimization_barrier(jnp.mean(tensor * tensor, axis=-1, keepdims=True)) + norm_eps)
    return tensor * inv_rms * gain_row.reshape(HEADS, HD)

def reference(noise, plan, slides, w_in, w_mod, w_qkv, qk_gain, w_o, w_out):
    window = STEPS_DEV * N_SLAB

    def one_pair(operands):
        q_pair, k_pair, v_pair = operands
        scores = jnp.dot(q_pair, k_pair.T, preferred_element_type=jnp.float32) * HD ** (-0.5)
        row_max = lax.optimization_barrier(jnp.max(scores, axis=-1, keepdims=True))
        lifted = jnp.exp(scores - row_max)
        row_total = lax.optimization_barrier(jnp.sum(lifted, axis=-1, keepdims=True))
        weights_bf = (lifted / row_total).astype(jnp.bfloat16)
        return jnp.dot(weights_bf, v_pair, preferred_element_type=jnp.float32).astype(jnp.bfloat16)

    def drift(operands):
        state, level = operands
        embedded = jnp.einsum('cpt,pd->ctd', rounded(state), w_in.astype(jnp.float32))
        features = time_features(level[None], FREQ).astype(jnp.bfloat16)
        modulation = jnp.dot(features, w_mod, preferred_element_type=jnp.float32)[0]
        normed = layer_norm(embedded) * (1.0 + modulation[:D]) + modulation[D:]
        joined = jnp.einsum('ctd,de->cte', rounded(normed), w_qkv.astype(jnp.float32))
        queries = head_norm(joined[..., :D].reshape(CLIPS, TOKENS, HEADS, HD), qk_gain[0]).astype(jnp.bfloat16)
        key_part = head_norm(joined[..., D:2 * D].reshape(CLIPS, TOKENS, HEADS, HD), qk_gain[1]).astype(jnp.bfloat16)
        value_part = joined[..., 2 * D:].reshape(CLIPS, TOKENS, HEADS, HD).astype(jnp.bfloat16)

        def by_pair(tensor):
            return tensor.transpose(0, 2, 1, 3).reshape(CLIPS * HEADS, TOKENS, HD)
        attended = lax.map(one_pair, (by_pair(queries), by_pair(key_part), by_pair(value_part)))
        merged = attended.reshape(CLIPS, HEADS, TOKENS, HD).transpose(0, 2, 1, 3).reshape(CLIPS, TOKENS, D)
        mixed = embedded + jnp.einsum('ctd,de->cte', merged.astype(jnp.float32), w_o.astype(jnp.float32))
        return jnp.einsum('ctd,dp->cpt', rounded(layer_norm(mixed)), w_out.astype(jnp.float32))
    anchor = noise
    states = jnp.broadcast_to(anchor[None], (window,) + anchor.shape)
    offset = jnp.zeros((), jnp.int32)
    for sweep_index in range(SWEEPS):
        levels = lax.dynamic_slice_in_dim(plan, offset, window + 1).astype(jnp.float32)
        step_size = (levels[1:] - levels[:-1]) / 1000.0
        velocity = lax.map(drift, (states, levels[:-1]))
        terms = step_size[:, None, None, None] * velocity
        earlier = jnp.concatenate([jnp.zeros_like(terms[:1]), jnp.cumsum(terms[:-1], axis=0)], axis=0)
        states = anchor[None] + earlier
        final_state = anchor + lax.optimization_barrier(jnp.sum(terms, axis=0))
        shift_by = slides[sweep_index]
        extended = jnp.concatenate([states, jnp.broadcast_to(final_state[None], states.shape)], axis=0)
        states = lax.dynamic_slice_in_dim(extended, shift_by, window)
        anchor = states[0]
        offset = offset + shift_by
    return (states, anchor)
```

```python
import functools
import math

import jax
import jax.numpy as jnp
import numpy as np
from jax import lax
from jax.experimental import pallas as pl
from jax.experimental.pallas import tpu as pltpu
from jax.sharding import PartitionSpec as P

HEADS = 16
HD = 72
STEPS_DEV = 2
SWEEPS = 2
PATCH = 16
FE = 24
LANES = 128
WIDTH = HEADS * HD
GROUPS = 4
WINDOW_LANES = 384

norm_eps = 1e-06
MESH = pl.DeviceIdType.MESH
f32 = jnp.float32
bf16 = jnp.bfloat16


def dot(a, b):
    return lax.dot_general(a, b, (((1,), (0,)), ((), ())), preferred_element_type=f32)


def dot_nt(a, b):
    return lax.dot_general(a, b, (((1,), (1,)), ((), ())), preferred_element_type=f32)


def split(x):
    high = x.astype(bf16)
    return high, (x - high.astype(f32)).astype(bf16)


def fold_kernel(m_ref, gain_ref, at_ref, bk_ref, bq_ref, mv_ref):
    lane = lax.broadcasted_iota(jnp.int32, (FE, LANES), 1)

    def three(x):
        high = x.astype(bf16).astype(f32)
        col = lax.broadcasted_iota(jnp.int32, x.shape, 1)
        return jnp.where((col >= FE) & (col < 2 * FE), x - high, high).astype(bf16)

    pad = jnp.zeros((LANES - 3 * FE, WINDOW_LANES), f32)
    for g in range(GROUPS):
        start = 256 * g
        mq = m_ref[0, :, start : start + WINDOW_LANES]
        mk = m_ref[0, :, WIDTH + start : WIDTH + start + WINDOW_LANES]
        mv = m_ref[0, :, 2 * WIDTH + start : 2 * WIDTH + start + WINDOW_LANES]
        gain = gain_ref[:, start : start + WINDOW_LANES]
        col = lax.broadcasted_iota(jnp.int32, (FE, WINDOW_LANES), 1) + start

        def block(x, rows_per_head):
            parts = []
            for p in range(4):
                h = 4 * g + p
                parts.append(jnp.where((col >= HD * h) & (col < HD * (h + 1)), x, 0.0))
                if rows_per_head > FE:
                    parts.append(jnp.zeros((rows_per_head - FE, WINDOW_LANES), f32))
            return jnp.concatenate(parts, axis=0)

        def product(left, right):
            lh, ll = split(block(left, FE))
            rh, rl = split(jnp.concatenate([right, right, right, pad], axis=0))
            out = dot_nt(
                jnp.concatenate([lh, ll], axis=0), jnp.concatenate([rh, rl], axis=0)
            )
            rows = 4 * FE
            return out[:rows, :LANES] + out[rows:, :LANES] + out[:rows, LANES:]

        rows = pl.ds(4 * FE * g, 4 * FE)
        bk_ref[0, rows, :] = three(product(mk, mk * (1.0 / HD)))
        bq_ref[0, rows, :] = three(product(mq, mq * (1.0 / HD)))
        a = three(product(mk * gain, mq)).astype(f32)
        for p in range(4):
            piece = a[FE * p : FE * (p + 1)]
            full = jnp.concatenate(
                [piece, piece, piece, jnp.zeros((LANES - 3 * FE, LANES), f32)], axis=0
            )
            at_ref[0, pl.ds(LANES * (4 * g + p), LANES), :] = full.astype(bf16)
        left = block(mv, 32)
        cols = []
        if start:
            cols.append(jnp.zeros((LANES, start), f32))
        cols.append(left)
        if start + WINDOW_LANES < WIDTH:
            cols.append(jnp.zeros((LANES, WIDTH - start - WINDOW_LANES), f32))
        mv_ref[0, pl.ds(LANES * g, LANES), :] = jnp.concatenate(cols, axis=1).astype(bf16)


def fold(m, gain):
    combos = m.shape[0]

    def spec(rows, cols):
        return pl.BlockSpec((1, rows, cols), lambda t: (t, 0, 0))

    return pl.pallas_call(
        fold_kernel,
        grid=(combos,),
        in_specs=[spec(FE, 3 * WIDTH), pl.BlockSpec((1, WIDTH), lambda t: (0, 0))],
        out_specs=[
            spec(HEADS * LANES, LANES),
            spec(HEADS * FE, LANES),
            spec(HEADS * FE, LANES),
            spec(HEADS * 32, WIDTH),
        ],
        out_shape=[
            jax.ShapeDtypeStruct((combos, HEADS * LANES, LANES), bf16),
            jax.ShapeDtypeStruct((combos, HEADS * FE, LANES), bf16),
            jax.ShapeDtypeStruct((combos, HEADS * FE, LANES), bf16),
            jax.ShapeDtypeStruct((combos, HEADS * 32, WIDTH), bf16),
        ],
        compiler_params=pltpu.CompilerParams(vmem_limit_bytes=32 << 20),
    )(m, gain)


def time_features(levels, feature_count):
    half_width = feature_count // 2
    frequency = jnp.exp(-math.log(10000.0) * jnp.arange(half_width, dtype=f32) / half_width)
    angles = levels[:, None] * frequency[None, :]
    return jnp.concatenate([jnp.cos(angles), jnp.sin(angles)], axis=-1)


def prepare(levels, w_in, w_mod, w_qkv, qk_gain):
    combos = levels.shape[0]
    features = time_features(levels, w_mod.shape[0]).astype(bf16)
    modulation = jnp.dot(features, w_mod, preferred_element_type=f32)
    wide = w_in.astype(f32)
    centered = wide - jnp.mean(wide, axis=1, keepdims=True)
    gram = lax.dot_general(
        centered, centered, (((1,), (1,)), ((), ())), precision=lax.Precision.HIGHEST
    ) * (1.0 / WIDTH)
    g1 = gram.astype(bf16)
    rest = gram - g1.astype(f32)
    g2 = rest.astype(bf16)
    g3 = (rest - g2.astype(f32)).astype(bf16)
    gram3 = jnp.concatenate([g1, g2, g3], axis=0)
    rows = jnp.concatenate(
        [
            centered[None] * (1.0 + modulation[:, None, :WIDTH]),
            modulation[:, None, WIDTH:],
            jnp.zeros((combos, FE - PATCH - 1, WIDTH), f32),
        ],
        axis=1,
    ).reshape(combos * FE, WIDTH)
    high, low = split(rows)
    both = jnp.dot(jnp.concatenate([high, low], axis=0), w_qkv, preferred_element_type=f32)
    m = (both[: combos * FE] + both[combos * FE :]).reshape(combos, FE, 3 * WIDTH)
    gain = (qk_gain[0] * qk_gain[1] * (HD**-0.5 * math.log2(math.e))).reshape(1, WIDTH)
    return gram3, fold(m, gain)


def features_of(x, gram):
    g = dot(gram, x.astype(bf16))
    t = g[:PATCH] + g[PATCH : 2 * PATCH] + g[2 * PATCH :]
    spread = jnp.sum(x * t, axis=0, keepdims=True)
    u = x * lax.rsqrt(jnp.maximum(spread, 0.0) + norm_eps)
    count = x.shape[1]
    first = lax.broadcasted_iota(jnp.int32, (FE - PATCH, count), 0) == 0
    u = jnp.concatenate([u, jnp.where(first, 1.0, 0.0)], axis=0)
    high = u.astype(bf16).astype(f32)
    low = u - high
    f = jnp.concatenate([high, high, low, jnp.zeros((LANES - 3 * FE, count), f32)], axis=0)
    return u, f.astype(bf16)


def head_scale(weights, u, f):
    t = dot(weights, f).reshape(HEADS, FE, f.shape[1])
    total = jnp.sum(t * u[None], axis=1)
    return lax.rsqrt(jnp.maximum(total, 0.0) + norm_eps)


def attend_kernel(
    step_ref, own_ref, all_ref, gram_ref, at_ref, bk_ref, bq_ref, mv_ref, wo_ref, win_ref,
    wout_ref, out_ref, xs, kf, rho, qs, scores, zs, att,
):
    sources, kinds = all_ref.shape[:2]
    tokens = sources * 64
    gram = gram_ref[...]
    chunk = 512
    lane = lax.broadcasted_iota(jnp.int32, (PATCH, LANES), 1)

    for s in range(STEPS_DEV):
        k = s % kinds
        if s < kinds:
            for p in range(sources // 2):
                a = all_ref[2 * p, k].astype(f32)
                b = all_ref[2 * p + 1, k].astype(f32)
                xs[:, pl.ds(LANES * p, LANES)] = jnp.where(lane < 64, a, pltpu.roll(b, 64, 1))
                xs[:, pl.ds(tokens + LANES * p, LANES)] = jnp.where(
                    lane < 64, pltpu.roll(a, 64, 1), b
                )

        @pl.loop(0, 2 * tokens // chunk)
        def _(n):
            cols = pl.ds(pl.multiple_of(n * chunk, chunk), chunk)
            u, f = features_of(xs[:, cols], gram)
            kf[:, cols] = f
            scale = head_scale(bk_ref[s], u, f)
            for g in range(GROUPS):
                rho[g, pl.ds(0, 4), cols] = scale[4 * g : 4 * g + 4]

        own = own_ref[k].astype(f32)
        u, f = features_of(own, gram)
        scale = head_scale(bq_ref[s], u, f)
        row = lax.broadcasted_iota(jnp.int32, (LANES, LANES), 0)
        for h in range(HEADS):
            q = dot(at_ref[s, pl.ds(LANES * h, LANES), :], f) * scale[h : h + 1]
            high = q.astype(bf16).astype(f32)
            q = jnp.where((row >= FE) & (row < 2 * FE), q - high, high).T
            for c in range(2):
                qs[c, pl.ds(64 * h, 64), :] = q[64 * c : 64 * (c + 1)].astype(bf16)

        lane64 = lax.broadcasted_iota(jnp.int32, (64, LANES), 1)
        for c in range(2):
            keys = pl.ds(tokens * c, tokens)

            @pl.loop(0, GROUPS)
            def _(g):
                sc = dot(qs[c, pl.ds(pl.multiple_of(g * 256, 256), 256), :], kf[:, keys])
                r = rho[g, pl.ds(0, 4), keys]
                sc = sc.reshape(4, 64, tokens) * r[:, None, :]
                sc = sc.reshape(256, tokens)
                top = jnp.max(sc, axis=1, keepdims=True)
                probs = jnp.exp2(sc - top).astype(bf16)
                o = dot_nt(probs, kf[:, keys])
                o = o + pltpu.roll(o, LANES - 2 * FE, 1)
                z = jnp.zeros((64, LANES), f32)
                for p in range(4):
                    piece = o[64 * p : 64 * (p + 1)]
                    piece = jnp.where(lane64 < FE, piece / piece[:, PATCH : PATCH + 1], 0.0)
                    z = z + (pltpu.roll(piece, 32 * p, 1) if p else piece)
                zs[g, pl.ds(64 * c, 64), :] = z.astype(bf16)

        z = jnp.concatenate([zs[g] for g in range(GROUPS)], axis=1)
        att[pl.ds(LANES * s, LANES), :] = dot(z, mv_ref[s]).astype(bf16)

    for s in range(STEPS_DEV):
        k = s % kinds
        embedded = lax.dot_general(
            own_ref[k], win_ref[...], (((0,), (0,)), ((), ())), preferred_element_type=f32
        )
        mixed = embedded + dot(att[pl.ds(LANES * s, LANES), :], wo_ref[...])
        centered = mixed - jnp.mean(mixed, axis=1, keepdims=True)
        spread = jnp.mean(centered * centered, axis=1, keepdims=True)
        normed = (centered * lax.rsqrt(spread + norm_eps)).astype(bf16)
        out_ref[s] = dot_nt(wout_ref[...], normed) * step_ref[s]


def attend(step_size, own, everything, gram3, weights, w_o, w_in, w_out_t):
    at, bk, bq, mv = weights
    sources = everything.shape[0]
    tokens = sources * 64
    vmem = pl.BlockSpec(memory_space=pltpu.VMEM)
    return pl.pallas_call(
        attend_kernel,
        in_specs=[pl.BlockSpec(memory_space=pltpu.SMEM)] + [vmem] * 10,
        out_specs=vmem,
        out_shape=jax.ShapeDtypeStruct((STEPS_DEV, PATCH, LANES), f32),
        scratch_shapes=[
            pltpu.VMEM((PATCH, 2 * tokens), f32),
            pltpu.VMEM((LANES, 2 * tokens), bf16),
            pltpu.VMEM((GROUPS, 8, 2 * tokens), f32),
            pltpu.VMEM((2, HEADS * 64, LANES), bf16),
            pltpu.VMEM((256, tokens), f32),
            pltpu.VMEM((GROUPS, LANES, LANES), bf16),
            pltpu.VMEM((2 * LANES, WIDTH), bf16),
        ],
        compiler_params=pltpu.CompilerParams(vmem_limit_bytes=48 << 20),
    )(step_size, own, everything, gram3, at, bk, bq, mv, w_o, w_in, w_out_t)


def greet(axes):
    barrier = pltpu.get_barrier_semaphore()
    total = 0
    for axis, count in axes:
        me = lax.axis_index(axis)

        @pl.loop(1, count)
        def _(i):
            pl.semaphore_signal(
                barrier, inc=1, device_id={axis: lax.rem(me + i, count)}, device_id_type=MESH
            )

        total += count - 1
    pl.semaphore_wait(barrier, total)


def spread_to(axis, count, src, dst, send, recv, local):
    me = lax.axis_index(axis)

    def copy(i, place):
        return pltpu.make_async_remote_copy(
            src_ref=src,
            dst_ref=dst.at[place],
            send_sem=send.at[i],
            recv_sem=recv.at[i],
            device_id={axis: lax.rem(me + i, count)},
            device_id_type=MESH,
        )

    @pl.loop(1, count)
    def _(i):
        copy(i, me).start()

    here = pltpu.make_async_copy(src, dst.at[me], local)
    here.start()
    here.wait()

    @pl.loop(1, count)
    def _(i):
        copy(i, lax.rem(me + count - i, count)).wait()


def gather_kernel(count, x_ref, out_ref, send, recv, local):
    greet((("seq", count),))
    spread_to("seq", count, x_ref, out_ref, send, recv, local)


def gather(x, count):
    vmem = pl.BlockSpec(memory_space=pltpu.VMEM)
    return pl.pallas_call(
        functools.partial(gather_kernel, count),
        in_specs=[vmem],
        out_specs=vmem,
        out_shape=jax.ShapeDtypeStruct((count,) + x.shape, x.dtype),
        scratch_shapes=[
            pltpu.SemaphoreType.DMA((count,)),
            pltpu.SemaphoreType.DMA((count,)),
            pltpu.SemaphoreType.DMA,
        ],
        compiler_params=pltpu.CompilerParams(collective_id=1, has_side_effects=True),
    )(x)


def picard(first, shift, anchor, terms_ref, slabs):
    steps = STEPS_DEV * slabs
    state = [anchor] * (STEPS_DEV + 1)
    limits = [first + a for a in range(STEPS_DEV)] + [shift]
    for j in range(steps):
        term = terms_ref[j // STEPS_DEV, j % STEPS_DEV]
        state = [v + jnp.where(j < n, term, 0.0) for v, n in zip(state, limits)]
    return state


def slide_kernel(
    slabs, count, shift_ref, terms_ref, anchor_ref, own_ref, new_anchor_ref, all_ref,
    every, send_a, recv_a, send_b, recv_b, local,
):
    greet((("slab", slabs), ("seq", count)))
    spread_to("slab", slabs, terms_ref, every, send_a, recv_a, local.at[0])
    shift = shift_ref[0]
    first = STEPS_DEV * lax.axis_index("slab") + shift
    state = picard(first, shift, anchor_ref[...], every, slabs)
    for a in range(STEPS_DEV):
        own_ref[a] = state[a].astype(bf16)
    new_anchor_ref[...] = state[-1]
    spread_to("seq", count, own_ref, all_ref, send_b, recv_b, local.at[1])


def slide(shift, terms, anchor, slabs, count):
    vmem = pl.BlockSpec(memory_space=pltpu.VMEM)
    return pl.pallas_call(
        functools.partial(slide_kernel, slabs, count),
        in_specs=[pl.BlockSpec(memory_space=pltpu.SMEM), vmem, vmem],
        out_specs=[vmem] * 3,
        out_shape=[
            jax.ShapeDtypeStruct(terms.shape, bf16),
            jax.ShapeDtypeStruct(anchor.shape, f32),
            jax.ShapeDtypeStruct((count,) + terms.shape, bf16),
        ],
        scratch_shapes=[
            pltpu.VMEM((slabs,) + terms.shape, f32),
            pltpu.SemaphoreType.DMA((slabs,)),
            pltpu.SemaphoreType.DMA((slabs,)),
            pltpu.SemaphoreType.DMA((count,)),
            pltpu.SemaphoreType.DMA((count,)),
            pltpu.SemaphoreType.DMA((2,)),
        ],
        compiler_params=pltpu.CompilerParams(collective_id=2, has_side_effects=True),
    )(shift, terms, anchor)


def finish_kernel(slabs, shift_ref, terms_ref, anchor_ref, out_ref, new_anchor_ref, every, send, recv, local):
    greet((("slab", slabs),))
    spread_to("slab", slabs, terms_ref, every, send, recv, local)
    shift = shift_ref[0]
    first = STEPS_DEV * lax.axis_index("slab") + shift
    state = picard(first, shift, anchor_ref[...], every, slabs)
    for a in range(STEPS_DEV):
        out_ref[a] = state[a]
    new_anchor_ref[...] = state[-1]


def finish(shift, terms, anchor, slabs):
    vmem = pl.BlockSpec(memory_space=pltpu.VMEM)
    return pl.pallas_call(
        functools.partial(finish_kernel, slabs),
        in_specs=[pl.BlockSpec(memory_space=pltpu.SMEM), vmem, vmem],
        out_specs=[vmem] * 2,
        out_shape=[
            jax.ShapeDtypeStruct(terms.shape, f32),
            jax.ShapeDtypeStruct(anchor.shape, f32),
        ],
        scratch_shapes=[
            pltpu.VMEM((slabs,) + terms.shape, f32),
            pltpu.SemaphoreType.DMA((slabs,)),
            pltpu.SemaphoreType.DMA((slabs,)),
            pltpu.SemaphoreType.DMA,
        ],
        compiler_params=pltpu.CompilerParams(collective_id=3, has_side_effects=True),
    )(shift, terms, anchor)


def on_device(noise, plan, slides, w_in, w_mod, w_qkv, qk_gain, w_o, w_out):
    slabs, count = lax.axis_size("slab"), lax.axis_size("seq")
    anchor = jnp.concatenate([noise[0], noise[1]], axis=-1)
    own = anchor.astype(bf16)[None]
    everything = gather(own, count)
    first = STEPS_DEV * lax.axis_index("slab")
    levels, sizes = [], []
    for offset in (jnp.zeros((), jnp.int32), slides[0]):
        part = lax.dynamic_slice_in_dim(plan, offset + first, STEPS_DEV + 1).astype(f32)
        levels.append(part[:-1])
        sizes.append((part[1:] - part[:-1]) / 1000.0)
    gram3, weights = prepare(jnp.concatenate(levels), w_in, w_mod, w_qkv, qk_gain)
    w_out_t = w_out.T
    for sweep in range(SWEEPS):
        mine = [w[STEPS_DEV * sweep : STEPS_DEV * (sweep + 1)] for w in weights]
        terms = attend(sizes[sweep], own, everything, gram3, mine, w_o, w_in, w_out_t)
        shift = slides[sweep : sweep + 1]
        if sweep + 1 < SWEEPS:
            own, anchor, everything = slide(shift, terms, anchor, slabs, count)
        else:
            states, anchor = finish(shift, terms, anchor, slabs)
    half = LANES // 2
    states = jnp.stack([states[..., :half], states[..., half:]], axis=1)
    anchor = jnp.stack([anchor[..., :half], anchor[..., half:]], axis=0)
    return (states, anchor)


def solution(mesh):
    return jax.shard_map(
        on_device,
        mesh=mesh,
        in_specs=(P(None, None, "seq"), P(), P(), P(), P(), P(), P(), P(), P()),
        out_specs=(P("slab", None, None, "seq"), P(None, None, "seq")),
        check_vma=False,
    )
```

```python
import math

import jax
import jax.numpy as jnp
import numpy as np
from jax import lax
from jax.experimental import pallas as pl
from jax.experimental.pallas import tpu as pltpu
from jax.sharding import PartitionSpec as P

HEADS = 16
HD = 72
STEPS_DEV = 2
SWEEPS = 2
COMBOS = STEPS_DEV * SWEEPS
CLIPS = 2
PATCH = 16
FREQ = 256
FE = 24
LANES = 128
OWN = 64
WIDTH = HEADS * HD
GROUPS = 4
WINDOW_LANES = 384
HB = 8
ROWS = HB * OWN
SUB = 16
CHUNK = 1024

norm_eps = 1e-06
MESH = pl.DeviceIdType.MESH
f32 = jnp.float32
bf16 = jnp.bfloat16


def dot(a, b):
    return lax.dot_general(a, b, (((1,), (0,)), ((), ())), preferred_element_type=f32)


def dot_nt(a, b):
    return lax.dot_general(a, b, (((1,), (1,)), ((), ())), preferred_element_type=f32)


def split(x):
    high = x.astype(bf16)
    return high, (x - high.astype(f32)).astype(bf16)


def modulated_rows(plan_ref, slides_ref, freq_ref, w_mod, w_in, gram, lhs):
    first = STEPS_DEV * lax.axis_index("slab")
    row = lax.broadcasted_iota(jnp.int32, (8, FREQ // 2), 0)
    level = jnp.zeros((8, FREQ // 2), f32)
    for t in range(COMBOS):
        place = first + t % STEPS_DEV
        if t >= STEPS_DEV:
            place = place + slides_ref[0]
        level = jnp.where(row == t, plan_ref[place].astype(f32), level)
    angles = level * freq_ref[...]
    features = jnp.concatenate([jnp.cos(angles), jnp.sin(angles)], axis=1).astype(bf16)
    modulation = dot(features, w_mod[...])
    wide = w_in[...].astype(f32)
    centered = wide - jnp.mean(wide, axis=1, keepdims=True)
    square = lax.dot_general(
        centered, centered, (((1,), (1,)), ((), ())),
        precision=lax.Precision.HIGHEST, preferred_element_type=f32,
    ) * (1.0 / WIDTH)
    g1 = square.astype(bf16)
    rest = square - g1.astype(f32)
    g2 = rest.astype(bf16)
    g3 = (rest - g2.astype(f32)).astype(bf16)
    for n, g in enumerate((g1, g2, g3)):
        gram[pl.ds(PATCH * n, PATCH), :] = g
    under = lax.broadcasted_iota(jnp.int32, (FE - PATCH, WIDTH), 0)
    rows = []
    for t in range(COMBOS):
        rows.append(centered * (1.0 + modulation[t : t + 1, :WIDTH]))
        rows.append(jnp.where(under == 0, modulation[t : t + 1, WIDTH:], 0.0))
    high, low = split(jnp.concatenate(rows, axis=0))
    lhs[pl.ds(0, COMBOS * FE), :] = high
    lhs[pl.ds(COMBOS * FE, COMBOS * FE), :] = low


def project(lhs, w_part, m_ref, part):
    @pl.loop(0, WIDTH // WINDOW_LANES)
    def _(n):
        at = pl.multiple_of(n * WINDOW_LANES, WINDOW_LANES)
        both = dot(lhs[...], w_part[:, pl.ds(at, WINDOW_LANES)])
        both = both[: COMBOS * FE] + both[COMBOS * FE :]
        to = pl.ds(pl.multiple_of(part * WIDTH + at, LANES), WINDOW_LANES)
        for t in range(COMBOS):
            m_ref[t, :, to] = both[FE * t : FE * (t + 1)]


def fold(t, m_ref, gain_ref, at_ref, bk_ref, bq_ref, mv_ref):
    def three(x):
        high = x.astype(bf16).astype(f32)
        col = lax.broadcasted_iota(jnp.int32, x.shape, 1)
        return jnp.where((col >= FE) & (col < 2 * FE), x - high, high).astype(bf16)

    pad = jnp.zeros((LANES - 3 * FE, WINDOW_LANES), f32)
    both_gains = gain_ref[0:1, :] * gain_ref[1:2, :] * (HD**-0.5 * math.log2(math.e))
    for g in range(GROUPS):
        start = 256 * g
        mq = m_ref[t, :, start : start + WINDOW_LANES]
        mk = m_ref[t, :, WIDTH + start : WIDTH + start + WINDOW_LANES]
        mv = m_ref[t, :, 2 * WIDTH + start : 2 * WIDTH + start + WINDOW_LANES]
        gain = both_gains[:, start : start + WINDOW_LANES]
        col = lax.broadcasted_iota(jnp.int32, (FE, WINDOW_LANES), 1) + start

        def block(x, rows_per_head):
            parts = []
            for p in range(4):
                h = 4 * g + p
                parts.append(jnp.where((col >= HD * h) & (col < HD * (h + 1)), x, 0.0))
                if rows_per_head > FE:
                    parts.append(jnp.zeros((rows_per_head - FE, WINDOW_LANES), f32))
            return jnp.concatenate(parts, axis=0)

        def product(left, right):
            lh, ll = split(block(left, FE))
            rh, rl = split(jnp.concatenate([right, right, right, pad], axis=0))
            out = dot_nt(
                jnp.concatenate([lh, ll], axis=0), jnp.concatenate([rh, rl], axis=0)
            )
            rows = 4 * FE
            return out[:rows, :LANES] + out[rows:, :LANES] + out[:rows, LANES:]

        rows = pl.ds(4 * FE * g, 4 * FE)
        bk_ref[t, rows, :] = three(product(mk, mk * (1.0 / HD)))
        bq_ref[t, rows, :] = three(product(mq, mq * (1.0 / HD)))
        a = three(product(mk * gain, mq)).astype(f32)
        for p in range(4):
            piece = a[FE * p : FE * (p + 1)]
            full = jnp.concatenate(
                [piece, piece, piece, jnp.zeros((LANES - 3 * FE, LANES), f32)], axis=0
            )
            at_ref[t, pl.ds(LANES * (4 * g + p), LANES), :] = full.astype(bf16)
        left = block(mv, 32)
        cols = []
        if start:
            cols.append(jnp.zeros((LANES, start), f32))
        cols.append(left)
        if start + WINDOW_LANES < WIDTH:
            cols.append(jnp.zeros((LANES, WIDTH - start - WINDOW_LANES), f32))
        mv_ref[t, pl.ds(LANES * g, LANES), :] = jnp.concatenate(cols, axis=1).astype(bf16)


def features_of(x, gram):
    g = dot(gram, x.astype(bf16))
    t = g[:PATCH] + g[PATCH : 2 * PATCH] + g[2 * PATCH :]
    spread = jnp.sum(x * t, axis=0, keepdims=True)
    u = x * lax.rsqrt(jnp.maximum(spread, 0.0) + norm_eps)
    count = x.shape[1]
    first = lax.broadcasted_iota(jnp.int32, (FE - PATCH, count), 0) == 0
    u = jnp.concatenate([u, jnp.where(first, 1.0, 0.0)], axis=0)
    high = u.astype(bf16).astype(f32)
    low = u - high
    f = jnp.concatenate([high, high, low, jnp.zeros((LANES - 3 * FE, count), f32)], axis=0)
    return u, f.astype(bf16)


def head_scale(weights, u, f):
    t = dot(weights, f).reshape(HEADS, FE, f.shape[1])
    total = jnp.sum(t * u[None], axis=1)
    return lax.rsqrt(jnp.maximum(total, 0.0) + norm_eps)


def own_queries(sweep, kinds, own_ref, gram, at_ref, bq_ref, qs):
    row = lax.broadcasted_iota(jnp.int32, (LANES, LANES), 0)
    for s in range(STEPS_DEV):
        t = STEPS_DEV * sweep + s
        if s < kinds:
            u, f = features_of(own_ref[s].astype(f32), gram)
        scale = head_scale(bq_ref[t], u, f)
        for h in range(HEADS):
            q = dot(at_ref[t, pl.ds(LANES * h, LANES), :], f) * scale[h : h + 1]
            high = q.astype(bf16).astype(f32)
            q = jnp.where((row >= FE) & (row < 2 * FE), q - high, high).T.astype(bf16)
            for c in range(CLIPS):
                lines = pl.ds(OWN * (h % HB), OWN)
                qs[CLIPS * s + c, h // HB, lines, :] = q[OWN * c : OWN * (c + 1)]


def all_keys(sweep, kinds, all_ref, gram, bk_ref, xs, kf, rho):
    sources = all_ref.shape[0]
    tokens = sources * OWN
    lane = lax.broadcasted_iota(jnp.int32, (PATCH, LANES), 1)
    for s in range(kinds):
        for p in range(sources // 2):
            a = all_ref[2 * p, s].astype(f32)
            b = all_ref[2 * p + 1, s].astype(f32)
            cols = pl.ds(LANES * p, LANES)
            xs[0, :, cols] = jnp.where(lane < OWN, a, pltpu.roll(b, OWN, 1))
            xs[1, :, cols] = jnp.where(lane < OWN, pltpu.roll(a, OWN, 1), b)

        @pl.loop(0, CLIPS)
        def _(c):
            for n in range(tokens // CHUNK):
                cols = pl.ds(n * CHUNK, CHUNK)
                u, f = features_of(xs[c, :, cols], gram)
                kf[CLIPS * s + c, :, cols] = f
                for v in range(s, STEPS_DEV, kinds):
                    scale = head_scale(bk_ref[STEPS_DEV * sweep + v], u, f)
                    for g in range(GROUPS):
                        rho[CLIPS * v + c, g, pl.ds(0, 4), cols] = scale[4 * g : 4 * g + 4]


def attend(kinds, tokens, qs, kf, rho, sc, pr, zs):
    lane = lax.broadcasted_iota(jnp.int32, (OWN, LANES), 1)
    parts = tokens // 256
    per = HEADS // HB
    blocks = CLIPS * STEPS_DEV * per

    def pair_of(block):
        pair = block // per
        return pair, pair % (CLIPS * kinds), block % per

    def stages(score, soft, value, slot):
        if score is not None:
            s_pair, s_keys, s_part = pair_of(score)
            q = qs[s_pair, s_part]
        if value is not None:
            v_pair, v_keys, v_part = pair_of(value)
            out = jnp.zeros((ROWS, LANES), f32)
        for n in range(parts):
            keys = pl.ds(256 * n, 256)
            if score is not None:
                t = dot(q, kf[s_keys, :, keys])
                for p in range(HB):
                    r = rho[s_pair, s_part * (HB // 4) + p // 4, pl.ds(p % 4, 1), keys]
                    sc[slot][pl.ds(OWN * p, OWN), keys] = t[OWN * p : OWN * (p + 1)] * r
            if soft is not None:
                some = ROWS // parts
                for m in range(some // SUB):
                    lines = pl.ds(some * n + SUB * m, SUB)
                    x = sc[1 - slot][lines, :]
                    x = x - jnp.max(x, axis=1, keepdims=True)
                    pr[1 - slot][lines, :] = jnp.exp2(x).astype(bf16)
            if value is not None:
                out = out + dot_nt(pr[slot][:, keys], kf[v_keys, :, keys])
        if value is not None:
            o = out + pltpu.roll(out, LANES - 2 * FE, 1)
            for g in range(HB // 4):
                z = jnp.zeros((OWN, LANES), f32)
                for p in range(4):
                    at = OWN * (4 * g + p)
                    piece = o[at : at + OWN]
                    piece = jnp.where(lane < FE, piece / piece[:, PATCH : PATCH + 1], 0.0)
                    z = z + (pltpu.roll(piece, 32 * p, 1) if p else piece)
                zs[v_pair, v_part * (HB // 4) + g] = z.astype(bf16)

    stages(0, None, None, 0)
    stages(1, 0, None, 1)

    @pl.loop(0, blocks // 2 - 1)
    def _(i):
        stages(2 * i + 2, 2 * i + 1, 2 * i, 0)
        stages(2 * i + 3, 2 * i + 2, 2 * i + 1, 1)

    stages(None, blocks - 1, blocks - 2, 0)
    stages(None, None, blocks - 1, 1)


def velocity_terms(sweep, kinds, sizes, own_ref, zs, mv_ref, w_o, w_in, w_out_t, out_ref):
    attended, embedded = [], []
    for s in range(STEPS_DEV):
        z = jnp.concatenate(
            [
                jnp.concatenate([zs[CLIPS * s + c, g] for g in range(GROUPS)], axis=1)
                for c in range(CLIPS)
            ],
            axis=0,
        )
        attended.append(dot(z, mv_ref[STEPS_DEV * sweep + s]).astype(bf16))
        embedded.append(
            lax.dot_general(
                own_ref[s % kinds], w_in[...], (((0,), (0,)), ((), ())),
                preferred_element_type=f32,
            )
        )
    mixed = jnp.concatenate(embedded, axis=0)
    mixed = mixed + dot(jnp.concatenate(attended, axis=0), w_o[...])
    centered = mixed - jnp.mean(mixed, axis=1, keepdims=True)
    spread = jnp.mean(centered * centered, axis=1, keepdims=True)
    normed = (centered * lax.rsqrt(spread + norm_eps)).astype(bf16)
    velocity = dot_nt(w_out_t[...], normed)
    for s in range(STEPS_DEV):
        out_ref[s] = velocity[:, LANES * s : LANES * (s + 1)] * sizes[s]


class Exchange:
    def __init__(self, axis, count, src, dst, send, recv):
        self.axis, self.count, self.src, self.dst = axis, count, src, dst
        self.send, self.recv = send, recv
        self.me = lax.axis_index(axis)

    def copy(self, i, place):
        return pltpu.make_async_remote_copy(
            src_ref=self.src,
            dst_ref=self.dst.at[place],
            send_sem=self.send.at[i],
            recv_sem=self.recv.at[i],
            device_id={self.axis: lax.rem(self.me + i, self.count)},
            device_id_type=MESH,
        )

    def start(self):
        @pl.loop(1, self.count)
        def _(i):
            self.copy(i, self.me).start()

        self.dst[self.me] = self.src[...]

    def wait(self):
        @pl.loop(1, self.count)
        def _(i):
            self.copy(i, lax.rem(self.me + self.count - i, self.count)).wait()


def greet(barrier, axis, count):
    me = lax.axis_index(axis)

    @pl.loop(1, count)
    def _(i):
        pl.semaphore_signal(
            barrier, inc=1, device_id={axis: lax.rem(me + i, count)}, device_id_type=MESH
        )


def picard(shift, anchor, terms_ref):
    slabs = terms_ref.shape[0]
    first = STEPS_DEV * lax.axis_index("slab") + shift
    limits = [first + a for a in range(STEPS_DEV)] + [shift]
    state = [anchor] * len(limits)
    for j in range(STEPS_DEV * slabs):
        term = terms_ref[j // STEPS_DEV, j % STEPS_DEV]
        state = [v + jnp.where(j < n, term, 0.0) for v, n in zip(state, limits)]
    return state


def window_kernel(
    plan_ref, slides_ref, freq_ref, noise_ref, w_in_hbm, w_mod_hbm, w_qkv_hbm, gain_hbm, w_o_hbm,
    w_out_hbm, states_ref, anchor_ref,
    noise, w_in, w_mod, wq, wk, wv, gain, w_o, w_out, load,
    lhs, m_ref, gram, at_ref, bk_ref, bq_ref, mv_ref, w_out_t,
    anchor, own0, own1, all0, all1, terms0, terms1, every0, every1,
    send0, recv0, send1, recv1, send2, recv2, send3, recv3,
    xs, kf, rho, qs, sc0, sc1, pr0, pr1, zs,
):
    slabs, count = every0.shape[0], all0.shape[0]
    tokens = count * OWN
    columns = [w_qkv_hbm.at[:, pl.ds(WIDTH * n, WIDTH)] for n in range(3)]
    pairs = (
        (noise_ref, noise), (w_in_hbm, w_in), (w_mod_hbm, w_mod), (columns[0], wq),
        (columns[1], wk), (columns[2], wv), (gain_hbm, gain), (w_out_hbm, w_out), (w_o_hbm, w_o),
    )
    loads = [pltpu.make_async_copy(a, b, load.at[n]) for n, (a, b) in enumerate(pairs)]
    for copy in loads:
        copy.start()
    barrier = pltpu.get_barrier_semaphore()
    greet(barrier, "seq", count)
    greet(barrier, "slab", slabs)

    loads[0].wait()
    start = jnp.concatenate([noise[0], noise[1]], axis=1)
    anchor[...] = start
    own0[0] = start.astype(bf16)
    loads[1].wait()
    loads[2].wait()
    modulated_rows(plan_ref, slides_ref, freq_ref, w_mod, w_in, gram, lhs)
    pl.semaphore_wait(barrier, count + slabs - 2)
    gather0 = Exchange("seq", count, own0, all0, send0, recv0)
    gather0.start()
    for n, part in enumerate((wq, wk, wv)):
        loads[3 + n].wait()
        project(lhs, part, m_ref, n)
    loads[6].wait()

    @pl.loop(0, COMBOS)
    def _(t):
        fold(t, m_ref, gain, at_ref, bk_ref, bq_ref, mv_ref)

    loads[7].wait()
    w_out_t[...] = w_out[...].astype(f32).T.astype(bf16)
    loads[8].wait()

    sc, pr = (sc0, sc1), (pr0, pr1)
    own, everyone = (own0, own1), (all0, all1)
    terms, every = (terms0, terms1), (every0, every1)
    sums = (
        Exchange("slab", slabs, terms0, every0, send1, recv1),
        Exchange("slab", slabs, terms1, every1, send3, recv3),
    )
    gather1 = Exchange("seq", count, own1, all1, send2, recv2)
    offset = 0
    for sweep in range(SWEEPS):
        kinds = own[sweep].shape[0]
        square = gram[...]
        own_queries(sweep, kinds, own[sweep], square, at_ref, bq_ref, qs)
        (gather0 if sweep == 0 else gather1).wait()
        all_keys(sweep, kinds, everyone[sweep], square, bk_ref, xs, kf, rho)
        attend(kinds, tokens, qs, kf, rho, sc, pr, zs)
        first = STEPS_DEV * lax.axis_index("slab") + offset
        levels = [plan_ref[first + a].astype(f32) for a in range(STEPS_DEV + 1)]
        sizes = [(levels[a + 1] - levels[a]) / 1000.0 for a in range(STEPS_DEV)]
        velocity_terms(
            sweep, kinds, sizes, own[sweep], zs, mv_ref, w_o, w_in, w_out_t, terms[sweep]
        )
        sums[sweep].start()
        sums[sweep].wait()
        shift = slides_ref[sweep]
        state = picard(shift, anchor[...], every[sweep])
        if sweep + 1 < SWEEPS:
            for a in range(STEPS_DEV):
                own1[a] = state[a].astype(bf16)
            gather1.start()
            anchor[...] = state[-1]
            offset = offset + shift
        else:
            for a in range(STEPS_DEV):
                for c in range(CLIPS):
                    states_ref[a, c] = state[a][:, OWN * c : OWN * (c + 1)]
            for c in range(CLIPS):
                anchor_ref[c] = state[-1][:, OWN * c : OWN * (c + 1)]


def on_device(noise, plan, slides, w_in, w_mod, w_qkv, qk_gain, w_o, w_out):
    slabs, count = lax.axis_size("slab"), lax.axis_size("seq")
    tokens = count * OWN
    half = FREQ // 2
    freq = np.exp(-math.log(10000.0) * np.arange(half) / half).astype(np.float32)[None]
    smem = pl.BlockSpec(memory_space=pltpu.SMEM)
    vmem = pl.BlockSpec(memory_space=pltpu.VMEM)
    far = pl.BlockSpec(memory_space=pl.ANY)
    block = (PATCH, LANES)

    def sems(n):
        return [pltpu.SemaphoreType.DMA((n,)), pltpu.SemaphoreType.DMA((n,))]

    return pl.pallas_call(
        window_kernel,
        in_specs=[smem, smem, vmem] + [far] * 7,
        out_specs=[vmem, vmem],
        out_shape=[
            jax.ShapeDtypeStruct((STEPS_DEV, CLIPS, PATCH, OWN), f32),
            jax.ShapeDtypeStruct((CLIPS, PATCH, OWN), f32),
        ],
        scratch_shapes=[
            pltpu.VMEM((CLIPS, PATCH, OWN), f32),
            pltpu.VMEM((PATCH, WIDTH), bf16),
            pltpu.VMEM((FREQ, 2 * WIDTH), bf16),
            pltpu.VMEM((WIDTH, WIDTH), bf16),
            pltpu.VMEM((WIDTH, WIDTH), bf16),
            pltpu.VMEM((WIDTH, WIDTH), bf16),
            pltpu.VMEM((2, WIDTH), f32),
            pltpu.VMEM((WIDTH, WIDTH), bf16),
            pltpu.VMEM((WIDTH, PATCH), bf16),
            pltpu.SemaphoreType.DMA((9,)),
            pltpu.VMEM((2 * COMBOS * FE, WIDTH), bf16),
            pltpu.VMEM((COMBOS, FE, 3 * WIDTH), f32),
            pltpu.VMEM((3 * PATCH, PATCH), bf16),
            pltpu.VMEM((COMBOS, HEADS * LANES, LANES), bf16),
            pltpu.VMEM((COMBOS, HEADS * FE, LANES), bf16),
            pltpu.VMEM((COMBOS, HEADS * FE, LANES), bf16),
            pltpu.VMEM((COMBOS, HEADS * 32, WIDTH), bf16),
            pltpu.VMEM((PATCH, WIDTH), bf16),
            pltpu.VMEM(block, f32),
            pltpu.VMEM((1,) + block, bf16),
            pltpu.VMEM((STEPS_DEV,) + block, bf16),
            pltpu.VMEM((count, 1) + block, bf16),
            pltpu.VMEM((count, STEPS_DEV) + block, bf16),
            pltpu.VMEM((STEPS_DEV,) + block, f32),
            pltpu.VMEM((STEPS_DEV,) + block, f32),
            pltpu.VMEM((slabs, STEPS_DEV) + block, f32),
            pltpu.VMEM((slabs, STEPS_DEV) + block, f32),
            *sems(count), *sems(slabs), *sems(count), *sems(slabs),
            pltpu.VMEM((CLIPS, PATCH, tokens), f32),
            pltpu.VMEM((CLIPS * STEPS_DEV, LANES, tokens), bf16),
            pltpu.VMEM((CLIPS * STEPS_DEV, GROUPS, 8, tokens), f32),
            pltpu.VMEM((CLIPS * STEPS_DEV, HEADS // HB, ROWS, LANES), bf16),
            pltpu.VMEM((ROWS, tokens), f32),
            pltpu.VMEM((ROWS, tokens), f32),
            pltpu.VMEM((ROWS, tokens), bf16),
            pltpu.VMEM((ROWS, tokens), bf16),
            pltpu.VMEM((CLIPS * STEPS_DEV, GROUPS, OWN, LANES), bf16),
        ],
        compiler_params=pltpu.CompilerParams(
            collective_id=1, has_side_effects=True, vmem_limit_bytes=56 << 20
        ),
    )(plan, slides, freq, noise, w_in, w_mod, w_qkv, qk_gain, w_o, w_out)


def solution(mesh):
    return jax.shard_map(
        on_device,
        mesh=mesh,
        in_specs=(P(None, None, "seq"), P(), P(), P(), P(), P(), P(), P(), P()),
        out_specs=(P("slab", None, None, "seq"), P(None, None, "seq")),
        check_vma=False,
    )
```

```python
import math

import jax
import jax.numpy as jnp
import numpy as np
from jax import lax
from jax.experimental import pallas as pl
from jax.experimental.pallas import tpu as pltpu
from jax.sharding import PartitionSpec as P

HEADS = 16
HD = 72
STEPS_DEV = 2
SWEEPS = 2
COMBOS = STEPS_DEV * SWEEPS
CLIPS = 2
PATCH = 16
FREQ = 256
FE = 24
LANES = 128
OWN = 64
WIDTH = HEADS * HD
GROUPS = 4
WINDOW_LANES = 384
WIDE = 640
TERMS = PATCH + 1
HB = 8
ROWS = HB * OWN
SUB = 16
CHUNK = 1024

norm_eps = 1e-06
MESH = pl.DeviceIdType.MESH
f32 = jnp.float32
bf16 = jnp.bfloat16


def dot(a, b):
    return lax.dot_general(a, b, (((1,), (0,)), ((), ())), preferred_element_type=f32)


def dot_nt(a, b):
    return lax.dot_general(a, b, (((1,), (1,)), ((), ())), preferred_element_type=f32)


def split(x):
    high = x.astype(bf16)
    return high, (x - high.astype(f32)).astype(bf16)


def modulated_rows(plan_ref, slides_ref, freq_ref, w_mod, w_in, gram, lhs):
    first = STEPS_DEV * lax.axis_index("slab")
    row = lax.broadcasted_iota(jnp.int32, (8, FREQ // 2), 0)
    level = jnp.zeros((8, FREQ // 2), f32)
    for t in range(COMBOS):
        place = first + t % STEPS_DEV
        if t >= STEPS_DEV:
            place = place + slides_ref[0]
        level = jnp.where(row == t, plan_ref[place].astype(f32), level)
    angles = level * freq_ref[...]
    features = jnp.concatenate([jnp.cos(angles), jnp.sin(angles)], axis=1).astype(bf16)
    modulation = dot(features, w_mod[...])
    wide = w_in[...].astype(f32)
    centered = wide - jnp.mean(wide, axis=1, keepdims=True)
    square = lax.dot_general(
        centered, centered, (((1,), (1,)), ((), ())),
        precision=lax.Precision.HIGHEST, preferred_element_type=f32,
    ) * (1.0 / WIDTH)
    g1 = square.astype(bf16)
    rest = square - g1.astype(f32)
    g2 = rest.astype(bf16)
    g3 = (rest - g2.astype(f32)).astype(bf16)
    for n, g in enumerate((g1, g2, g3)):
        gram[pl.ds(PATCH * n, PATCH), :] = g
    under = lax.broadcasted_iota(jnp.int32, (FE - PATCH, WIDTH), 0)
    rows = []
    for t in range(COMBOS):
        rows.append(centered * (1.0 + modulation[t : t + 1, :WIDTH]))
        rows.append(jnp.where(under == 0, modulation[t : t + 1, WIDTH:], 0.0))
    high, low = split(jnp.concatenate(rows, axis=0))
    lhs[pl.ds(0, COMBOS * FE), :] = high
    lhs[pl.ds(COMBOS * FE, COMBOS * FE), :] = low


def project(lhs, w_part, m_ref, part):
    @pl.loop(0, WIDTH // WINDOW_LANES)
    def _(n):
        at = pl.multiple_of(n * WINDOW_LANES, WINDOW_LANES)
        both = dot(lhs[...], w_part[:, pl.ds(at, WINDOW_LANES)])
        both = both[: COMBOS * FE] + both[COMBOS * FE :]
        to = pl.ds(pl.multiple_of(part * WIDTH + at, LANES), WINDOW_LANES)
        for t in range(COMBOS):
            m_ref[t, :, to] = both[FE * t : FE * (t + 1)]


def three(x):
    high = x.astype(bf16).astype(f32)
    col = lax.broadcasted_iota(jnp.int32, x.shape, 1)
    return jnp.where((col >= FE) & (col < 2 * FE), x - high, high)


def product(left, right):
    pad = jnp.zeros((LANES - 3 * FE, right.shape[1]), f32)
    right = jnp.concatenate([right, right, right, pad], axis=0)
    high, top = left.astype(bf16).astype(f32), right.astype(bf16).astype(f32)
    out = dot_nt(
        jnp.concatenate([high, left - high], axis=0).astype(bf16),
        jnp.concatenate([top, right - top], axis=0).astype(bf16),
    )
    rows = left.shape[0]
    return three(out[:rows, :LANES] + out[rows:, :LANES] + out[:rows, LANES:])


def norm_weights(t, part, m_ref, out_ref):
    pieces = []
    for g in range(2):
        start = 512 * g
        x = m_ref[t, :, part * WIDTH + start : part * WIDTH + start + WIDE]
        col = lax.broadcasted_iota(jnp.int32, (8, WIDE), 1) + start
        head = lax.broadcasted_iota(jnp.int32, (8, WIDE), 0) + 8 * g
        inside = (col >= HD * head) & (col < HD * (head + 1))
        left = [jnp.where(inside, x[e : e + 1], 0.0) for e in range(TERMS)]
        out = product(jnp.concatenate(left, axis=0), x * (1.0 / HD))
        pieces.append(out.reshape(TERMS, 8, LANES))
    both = jnp.concatenate(pieces, axis=1)
    out_ref[t] = both.reshape(TERMS * HEADS, LANES).astype(bf16)


def fold(t, m_ref, gain_ref, at_ref, bk_ref, bq_ref, mv_ref):
    norm_weights(t, 0, m_ref, bq_ref)
    norm_weights(t, 1, m_ref, bk_ref)
    both_gains = gain_ref[0:1, :] * gain_ref[1:2, :] * (HD**-0.5 * math.log2(math.e))
    for g in range(GROUPS):
        start = 256 * g
        mq = m_ref[t, :, start : start + WINDOW_LANES]
        mk = m_ref[t, :, WIDTH + start : WIDTH + start + WINDOW_LANES]
        mk = mk * both_gains[:, start : start + WINDOW_LANES]
        col = lax.broadcasted_iota(jnp.int32, (FE, WINDOW_LANES), 1) + start
        left = []
        for p in range(4):
            h = 4 * g + p
            left.append(jnp.where((col >= HD * h) & (col < HD * (h + 1)), mk, 0.0))
        a = product(jnp.concatenate(left, axis=0), mq)
        for p in range(4):
            piece = a[FE * p : FE * (p + 1)]
            full = jnp.concatenate(
                [piece, piece, piece, jnp.zeros((LANES - 3 * FE, LANES), f32)], axis=0
            )
            at_ref[t, pl.ds(LANES * (4 * g + p), LANES), :] = full.astype(bf16)
    for g in range(2):
        start = 512 * g
        mv = m_ref[t, :, 2 * WIDTH + start : 2 * WIDTH + start + WIDE]
        mv = jnp.concatenate([mv, jnp.zeros((32 - FE, WIDE), f32)], axis=0)
        col = lax.broadcasted_iota(jnp.int32, (32, WIDE), 1) + start
        for p in range(8):
            h = 8 * g + p
            inside = (col >= HD * h) & (col < HD * (h + 1))
            mv_ref[t, g, pl.ds(32 * p, 32), :] = jnp.where(inside, mv, 0.0).astype(bf16)


def features_of(x, gram):
    g = dot(gram, x.astype(bf16))
    t = g[:PATCH] + g[PATCH : 2 * PATCH] + g[2 * PATCH :]
    spread = jnp.sum(x * t, axis=0, keepdims=True)
    u = x * lax.rsqrt(jnp.maximum(spread, 0.0) + norm_eps)
    count = x.shape[1]
    first = lax.broadcasted_iota(jnp.int32, (FE - PATCH, count), 0) == 0
    u = jnp.concatenate([u, jnp.where(first, 1.0, 0.0)], axis=0)
    high = u.astype(bf16).astype(f32)
    low = u - high
    f = jnp.concatenate([high, high, low, jnp.zeros((LANES - 3 * FE, count), f32)], axis=0)
    return u, f.astype(bf16)


def head_scale(weights, u, f):
    t = dot(weights, f)
    total = t[:HEADS] * u[:1]
    for e in range(1, TERMS):
        total = total + t[HEADS * e : HEADS * (e + 1)] * u[e : e + 1]
    return lax.rsqrt(jnp.maximum(total, 0.0) + norm_eps)


def own_queries(sweep, own, gram, at_ref, bq_ref, qs):
    row = lax.broadcasted_iota(jnp.int32, (LANES, LANES), 0)
    left = lax.broadcasted_iota(jnp.int32, (1, LANES), 1) < OWN
    t = STEPS_DEV * sweep
    u, f = features_of(own.astype(f32), gram)
    scale = jnp.where(left, head_scale(bq_ref[t], u, f), head_scale(bq_ref[t + 1], u, f))
    for h in range(HEADS):
        lines = pl.ds(LANES * h, LANES)
        q = jnp.where(left, dot(at_ref[t, lines, :], f), dot(at_ref[t + 1, lines, :], f))
        q = q * scale[h : h + 1]
        high = q.astype(bf16).astype(f32)
        q = jnp.where((row >= FE) & (row < 2 * FE), q - high, high).T.astype(bf16)
        for s in range(STEPS_DEV):
            qs[s, h // HB, pl.ds(OWN * (h % HB), OWN), :] = q[OWN * s : OWN * (s + 1)]


def halves(all_ref, xs):
    left = lax.broadcasted_iota(jnp.int32, (PATCH, LANES), 1) < OWN
    for p in range(all_ref.shape[0] // 2):
        a = all_ref[2 * p].astype(f32)
        b = all_ref[2 * p + 1].astype(f32)
        cols = pl.ds(LANES * p, LANES)
        xs[0, :, cols] = jnp.where(left, a, pltpu.roll(b, OWN, 1))
        xs[1, :, cols] = jnp.where(left, pltpu.roll(a, OWN, 1), b)


def keys_of(x_ref, gram, kf, scales):
    for n in range(x_ref.shape[1] // CHUNK):
        cols = pl.ds(n * CHUNK, CHUNK)
        u, f = features_of(x_ref[:, cols], gram)
        kf[:, cols] = f
        for weights, rho in scales:
            scale = head_scale(weights, u, f)
            for g in range(GROUPS):
                rho[g, pl.ds(0, 4), cols] = scale[4 * g : 4 * g + 4]


def stages(score, soft, value, tokens):
    lane = lax.broadcasted_iota(jnp.int32, (OWN, LANES), 1)
    parts = tokens // 256
    if value is not None:
        out = jnp.zeros((ROWS, LANES), f32)
    for n in range(parts):
        keys = pl.ds(256 * n, 256)
        if score is not None:
            t = dot(score["q"][...], score["kf"][:, keys])
            for p in range(HB):
                r = score["rho"][score["part"] * (HB // 4) + p // 4, pl.ds(p % 4, 1), keys]
                score["sc"][pl.ds(OWN * p, OWN), keys] = t[OWN * p : OWN * (p + 1)] * r
        if soft is not None:
            some = ROWS // parts
            for m in range(some // SUB):
                lines = pl.ds(some * n + SUB * m, SUB)
                x = soft["sc"][lines, :]
                x = x - jnp.max(x, axis=1, keepdims=True)
                soft["pr"][lines, :] = jnp.exp2(x).astype(bf16)
        if value is not None:
            out = out + dot_nt(value["pr"][:, keys], value["kf"][:, keys])
    if value is not None:
        o = out + pltpu.roll(out, LANES - 2 * FE, 1)
        for g in range(HB // 4):
            z = jnp.zeros((OWN, LANES), f32)
            for p in range(4):
                at = OWN * (4 * g + p)
                piece = o[at : at + OWN]
                piece = jnp.where(lane < FE, piece / piece[:, PATCH : PATCH + 1], 0.0)
                z = z + (pltpu.roll(piece, 32 * p, 1) if p else piece)
            value["zs"][value["part"] * (HB // 4) + g] = z.astype(bf16)


def velocity_terms(sweep, sizes, own_ref, zs, mv_ref, w_o, w_in, w_out_t, out_ref):
    attended = []
    for s in range(STEPS_DEV):
        t = STEPS_DEV * sweep + s
        a = dot(jnp.concatenate([zs[s, 0], zs[s, 1]], axis=1), mv_ref[t, 0])
        b = dot(jnp.concatenate([zs[s, 2], zs[s, 3]], axis=1), mv_ref[t, 1])
        a = [a[:, :512], a[:, 512:] + b[:, :LANES], b[:, LANES:]]
        attended.append(jnp.concatenate(a, axis=1).astype(bf16))
    embedded = lax.dot_general(
        own_ref[...], w_in[...], (((0,), (0,)), ((), ())), preferred_element_type=f32
    )
    mixed = embedded + dot(jnp.concatenate(attended, axis=0), w_o[...])
    centered = mixed - jnp.mean(mixed, axis=1, keepdims=True)
    spread = jnp.mean(centered * centered, axis=1, keepdims=True)
    normed = (centered * lax.rsqrt(spread + norm_eps)).astype(bf16)
    left = lax.broadcasted_iota(jnp.int32, (1, LANES), 1) < OWN
    out_ref[...] = dot_nt(w_out_t[...], normed) * jnp.where(left, sizes[0], sizes[1])


class Exchange:
    def __init__(self, axis, count, src, dst, send, recv):
        self.axis, self.count, self.src, self.dst = axis, count, src, dst
        self.send, self.recv = send, recv
        self.me = lax.axis_index(axis)

    def copy(self, i, place):
        return pltpu.make_async_remote_copy(
            src_ref=self.src,
            dst_ref=self.dst.at[place],
            send_sem=self.send.at[i],
            recv_sem=self.recv.at[i],
            device_id={self.axis: lax.rem(self.me + i, self.count)},
            device_id_type=MESH,
        )

    def start(self):
        @pl.loop(1, self.count)
        def _(i):
            self.copy(i, self.me).start()

        self.dst[self.me] = self.src[...]

    def wait(self):
        @pl.loop(1, self.count)
        def _(i):
            self.copy(i, lax.rem(self.me + self.count - i, self.count)).wait()


def greet(barrier, axis, count):
    me = lax.axis_index(axis)

    @pl.loop(1, count)
    def _(i):
        pl.semaphore_signal(
            barrier, inc=1, device_id={axis: lax.rem(me + i, count)}, device_id_type=MESH
        )


def picard(shift, anchor, terms_ref):
    half = lax.broadcasted_iota(jnp.int32, (1, LANES), 1) // OWN
    first = STEPS_DEV * lax.axis_index("slab") + shift
    state, new_anchor = anchor, anchor
    for k in range(terms_ref.shape[0]):
        term = terms_ref[k]
        turned = pltpu.roll(term, OWN, 1)
        here, there = STEPS_DEV * k + half, STEPS_DEV * k + 1 - half
        state = state + jnp.where(here < first + half, term, 0.0)
        state = state + jnp.where(there < first + half, turned, 0.0)
        new_anchor = new_anchor + jnp.where(here < shift, term, 0.0)
        new_anchor = new_anchor + jnp.where(there < shift, turned, 0.0)
    return state, new_anchor


def window_kernel(
    plan_ref, slides_ref, freq_ref, noise_ref, w_in_hbm, w_mod_hbm, w_qkv_hbm, gain_hbm, w_o_hbm,
    w_out_hbm, moved_ref,
    noise, w_in, w_mod, wq, wk, wv, gain, w_o, w_out_t, load,
    lhs, m_ref, gram, at_ref, bk_ref, bq_ref, mv_ref,
    anchor, moved, packed, own0, own1, all0, all1, terms, every,
    send0, recv0, send1, recv1, send2, recv2,
    xs, kf0, kf1, rho, qs, sc0, sc1, pr0, pr1, zs,
):
    slabs, count = every.shape[2], all0.shape[0]
    tokens = count * OWN
    columns = [w_qkv_hbm.at[:, pl.ds(WIDTH * n, WIDTH)] for n in range(3)]
    pairs = (
        (noise_ref, noise), (w_in_hbm, w_in), (w_mod_hbm, w_mod), (columns[0], wq),
        (columns[1], wk), (columns[2], wv), (gain_hbm, gain), (w_out_hbm, w_out_t),
        (w_o_hbm, w_o),
    )
    loads = [pltpu.make_async_copy(a, b, load.at[n]) for n, (a, b) in enumerate(pairs)]
    for copy in loads:
        copy.start()
    barrier = pltpu.get_barrier_semaphore()
    greet(barrier, "seq", count)
    greet(barrier, "slab", slabs)

    loads[0].wait()
    packed[...] = jnp.concatenate([noise[0], noise[1]], axis=1).astype(bf16)
    for c in range(CLIPS):
        anchor[c] = jnp.concatenate([noise[c], noise[c]], axis=1)
        moved[c] = jnp.zeros_like(anchor[c])
        own0[c] = anchor[c].astype(bf16)
    loads[1].wait()
    loads[2].wait()
    modulated_rows(plan_ref, slides_ref, freq_ref, w_mod, w_in, gram, lhs)
    pl.semaphore_wait(barrier, count + slabs - 2)
    gather0 = Exchange("seq", count, packed, all0, send0, recv0)
    gather0.start()
    for n, part in enumerate((wq, wk, wv)):
        loads[3 + n].wait()
        project(lhs, part, m_ref, n)
    loads[6].wait()

    @pl.loop(0, STEPS_DEV)
    def _(t):
        fold(t, m_ref, gain, at_ref, bk_ref, bq_ref, mv_ref)

    loads[7].wait()
    loads[8].wait()

    square = gram[...]
    own = (own0, own1)
    per = HEADS // HB
    gathers = [
        Exchange("seq", count, own1.at[c], all1.at[c], send2.at[c], recv2.at[c])
        for c in range(CLIPS)
    ]
    sums = [
        [
            Exchange(
                "slab", slabs, terms.at[w, c], every.at[w, c], send1.at[w, c], recv1.at[w, c]
            )
            for c in range(CLIPS)
        ]
        for w in range(SWEEPS)
    ]

    def queries(w, c):
        own_queries(w, own[w][c], square, at_ref, bq_ref, qs.at[c])

    def finish(w, c):
        first = STEPS_DEV * lax.axis_index("slab")
        if w:
            first = first + slides_ref[0]
        levels = [plan_ref[first + a].astype(f32) for a in range(STEPS_DEV + 1)]
        sizes = [(levels[a + 1] - levels[a]) / 1000.0 for a in range(STEPS_DEV)]
        velocity_terms(
            w, sizes, own[w].at[c], zs.at[c], mv_ref, w_o, w_in, w_out_t, terms.at[w, c]
        )

    def send(w, c):
        sums[w][c].start()

    def slide(w, c):
        sums[w][c].wait()
        return picard(slides_ref[w], moved[c], every.at[w, c])

    def advance(c):
        state, moved[c] = slide(0, c)
        own1[c] = (anchor[c] + state).astype(bf16)
        gathers[c].start()

    def receive(c):
        gathers[c].wait()
        halves(all1.at[c], xs)
        for s in range(STEPS_DEV):
            scales = [(bk_ref[STEPS_DEV + s], rho.at[c, s])]
            keys_of(xs.at[s], square, kf1.at[c, s], scales)

    blocks = []
    for w in range(SWEEPS):
        for c in range(CLIPS):
            for s in range(STEPS_DEV):
                for part in range(per):
                    slot = len(blocks) % 2
                    blocks.append(
                        dict(
                            q=qs.at[c, s, part], kf=kf1.at[c, s] if w else kf0.at[c],
                            rho=rho.at[c, s], part=part, sc=(sc0, sc1)[slot],
                            pr=(pr0, pr1)[slot], zs=zs.at[c, s],
                        )
                    )
    one = STEPS_DEV * per
    turn = CLIPS * one

    def stage(n, low, high):
        def pick(k):
            return blocks[k] if low <= k < high else None

        stages(pick(n), pick(n - 1), pick(n - 2), tokens)

    for c in range(CLIPS):
        queries(0, c)
    gather0.wait()
    halves(all0, xs)
    for c in range(CLIPS):
        scales = [(bk_ref[s], rho.at[c, s]) for s in range(STEPS_DEV)]
        keys_of(xs.at[c], square, kf0.at[c], scales)
    for n in range(turn + 2):
        stage(n, 0, turn)
        if n == one + 1:
            finish(0, 0)
            send(0, 0)
        if n == turn:
            advance(0)
    finish(0, 1)
    send(0, 1)

    @pl.loop(STEPS_DEV, COMBOS)
    def _(t):
        fold(t, m_ref, gain, at_ref, bk_ref, bq_ref, mv_ref)

    queries(1, 0)
    advance(1)
    receive(0)
    for n in range(turn, 2 * turn + 2):
        if n == turn + one:
            queries(1, 1)
            receive(1)
        stage(n, turn, 2 * turn)
        if n == turn + one + 1:
            finish(1, 0)
        if n == turn + one + 2:
            send(1, 0)
    finish(1, 1)
    send(1, 1)
    for c in range(CLIPS):
        state, last = slide(1, c)
        for s in range(STEPS_DEV):
            moved_ref[s, c] = state[:, OWN * s : OWN * (s + 1)]
        moved_ref[STEPS_DEV, c] = last[:, :OWN]


def on_device(noise, plan, slides, w_in, w_mod, w_qkv, qk_gain, w_o, w_out):
    slabs, count = lax.axis_size("slab"), lax.axis_size("seq")
    tokens = count * OWN
    half = FREQ // 2
    freq = np.exp(-math.log(10000.0) * np.arange(half) / half).astype(np.float32)[None]
    smem = pl.BlockSpec(memory_space=pltpu.SMEM)
    vmem = pl.BlockSpec(memory_space=pltpu.VMEM)
    far = pl.BlockSpec(memory_space=pl.ANY)
    block = (PATCH, LANES)

    def sems(*shape):
        return [pltpu.SemaphoreType.DMA(shape), pltpu.SemaphoreType.DMA(shape)]

    moved = pl.pallas_call(
        window_kernel,
        in_specs=[smem, smem, vmem] + [far] * 7,
        out_specs=vmem,
        out_shape=jax.ShapeDtypeStruct((STEPS_DEV + 1, CLIPS, PATCH, OWN), f32),
        scratch_shapes=[
            pltpu.VMEM((CLIPS, PATCH, OWN), f32),
            pltpu.VMEM((PATCH, WIDTH), bf16),
            pltpu.VMEM((FREQ, 2 * WIDTH), bf16),
            pltpu.VMEM((WIDTH, WIDTH), bf16),
            pltpu.VMEM((WIDTH, WIDTH), bf16),
            pltpu.VMEM((WIDTH, WIDTH), bf16),
            pltpu.VMEM((2, WIDTH), f32),
            pltpu.VMEM((WIDTH, WIDTH), bf16),
            pltpu.VMEM((PATCH, WIDTH), bf16),
            pltpu.SemaphoreType.DMA((9,)),
            pltpu.VMEM((2 * COMBOS * FE, WIDTH), bf16),
            pltpu.VMEM((COMBOS, FE, 3 * WIDTH), f32),
            pltpu.VMEM((3 * PATCH, PATCH), bf16),
            pltpu.VMEM((COMBOS, HEADS * LANES, LANES), bf16),
            pltpu.VMEM((COMBOS, HEADS * TERMS, LANES), bf16),
            pltpu.VMEM((COMBOS, HEADS * TERMS, LANES), bf16),
            pltpu.VMEM((COMBOS, 2, HEADS * 16, WIDE), bf16),
            pltpu.VMEM((CLIPS,) + block, f32),
            pltpu.VMEM((CLIPS,) + block, f32),
            pltpu.VMEM(block, bf16),
            pltpu.VMEM((CLIPS,) + block, bf16),
            pltpu.VMEM((CLIPS,) + block, bf16),
            pltpu.VMEM((count,) + block, bf16),
            pltpu.VMEM((CLIPS, count) + block, bf16),
            pltpu.VMEM((SWEEPS, CLIPS) + block, f32),
            pltpu.VMEM((SWEEPS, CLIPS, slabs) + block, f32),
            *sems(count), *sems(SWEEPS, CLIPS, slabs), *sems(CLIPS, count),
            pltpu.VMEM((2, PATCH, tokens), f32),
            pltpu.VMEM((CLIPS, LANES, tokens), bf16),
            pltpu.VMEM((CLIPS, STEPS_DEV, LANES, tokens), bf16),
            pltpu.VMEM((CLIPS, STEPS_DEV, GROUPS, 8, tokens), f32),
            pltpu.VMEM((CLIPS, STEPS_DEV, HEADS // HB, ROWS, LANES), bf16),
            pltpu.VMEM((ROWS, tokens), f32),
            pltpu.VMEM((ROWS, tokens), f32),
            pltpu.VMEM((ROWS, tokens), bf16),
            pltpu.VMEM((ROWS, tokens), bf16),
            pltpu.VMEM((CLIPS, STEPS_DEV, GROUPS, OWN, LANES), bf16),
        ],
        compiler_params=pltpu.CompilerParams(
            collective_id=1, has_side_effects=True, vmem_limit_bytes=56 << 20
        ),
    )(plan, slides, freq, noise, w_in, w_mod, w_qkv, qk_gain, w_o, w_out.T)
    return noise[None] + moved[:STEPS_DEV], noise + moved[STEPS_DEV]


def solution(mesh):
    return jax.shard_map(
        on_device,
        mesh=mesh,
        in_specs=(P(None, None, "seq"), P(), P(), P(), P(), P(), P(), P(), P()),
        out_specs=(P("slab", None, None, "seq"), P(None, None, "seq")),
        check_vma=False,
    )
```

```python
import math

import jax
import jax.numpy as jnp
import numpy as np
from jax import lax
from jax.experimental import pallas as pl
from jax.experimental.pallas import tpu as pltpu
from jax.sharding import PartitionSpec as P

HEADS = 16
HD = 72
STEPS_DEV = 2
SWEEPS = 2
COMBOS = STEPS_DEV * SWEEPS
CLIPS = 2
PATCH = 16
FREQ = 256
FE = 24
LANES = 128
OWN = 64
WIDTH = HEADS * HD
GROUPS = 4
WINDOW_LANES = 384
WIDE = 640
TERMS = PATCH + 1
HB = 8
ROWS = HB * OWN
SUB = 16
CHUNK = 1024

norm_eps = 1e-06
MESH = pl.DeviceIdType.MESH
f32 = jnp.float32
bf16 = jnp.bfloat16


def dot(a, b):
    return lax.dot_general(a, b, (((1,), (0,)), ((), ())), preferred_element_type=f32)


def dot_nt(a, b):
    return lax.dot_general(a, b, (((1,), (1,)), ((), ())), preferred_element_type=f32)


def split(x):
    high = x.astype(bf16)
    return high, (x - high.astype(f32)).astype(bf16)


def modulated_rows(plan_ref, slides_ref, freq_ref, w_mod, w_in, gram, lhs):
    first = STEPS_DEV * lax.axis_index("slab")
    row = lax.broadcasted_iota(jnp.int32, (8, FREQ // 2), 0)
    level = jnp.zeros((8, FREQ // 2), f32)
    for t in range(COMBOS):
        place = first + t % STEPS_DEV
        if t >= STEPS_DEV:
            place = place + slides_ref[0]
        level = jnp.where(row == t, plan_ref[place].astype(f32), level)
    angles = level * freq_ref[...]
    features = jnp.concatenate([jnp.cos(angles), jnp.sin(angles)], axis=1).astype(bf16)
    modulation = dot(features, w_mod[...])
    wide = w_in[...].astype(f32)
    centered = wide - jnp.mean(wide, axis=1, keepdims=True)
    square = lax.dot_general(
        centered, centered, (((1,), (1,)), ((), ())),
        precision=lax.Precision.HIGHEST, preferred_element_type=f32,
    ) * (1.0 / WIDTH)
    g1 = square.astype(bf16)
    rest = square - g1.astype(f32)
    g2 = rest.astype(bf16)
    g3 = (rest - g2.astype(f32)).astype(bf16)
    for n, g in enumerate((g1, g2, g3)):
        gram[pl.ds(PATCH * n, PATCH), :] = g
    under = lax.broadcasted_iota(jnp.int32, (FE - PATCH, WIDTH), 0)
    rows = []
    for t in range(COMBOS):
        rows.append(centered * (1.0 + modulation[t : t + 1, :WIDTH]))
        rows.append(jnp.where(under == 0, modulation[t : t + 1, WIDTH:], 0.0))
    high, low = split(jnp.concatenate(rows, axis=0))
    lhs[pl.ds(0, COMBOS * FE), :] = high
    lhs[pl.ds(COMBOS * FE, COMBOS * FE), :] = low


def project(lhs, w_part, m_ref, part):
    @pl.loop(0, WIDTH // WINDOW_LANES)
    def _(n):
        at = pl.multiple_of(n * WINDOW_LANES, WINDOW_LANES)
        both = dot(lhs[...], w_part[:, pl.ds(at, WINDOW_LANES)])
        both = both[: COMBOS * FE] + both[COMBOS * FE :]
        to = pl.ds(pl.multiple_of(part * WIDTH + at, LANES), WINDOW_LANES)
        for t in range(COMBOS):
            m_ref[t, :, to] = both[FE * t : FE * (t + 1)]


def three(x):
    high = x.astype(bf16).astype(f32)
    col = lax.broadcasted_iota(jnp.int32, x.shape, 1)
    return jnp.where((col >= FE) & (col < 2 * FE), x - high, high)


def product(left, right):
    pad = jnp.zeros((LANES - 3 * FE, right.shape[1]), f32)
    right = jnp.concatenate([right, right, right, pad], axis=0)
    high, top = left.astype(bf16).astype(f32), right.astype(bf16).astype(f32)
    out = dot_nt(
        jnp.concatenate([high, left - high], axis=0).astype(bf16),
        jnp.concatenate([top, right - top], axis=0).astype(bf16),
    )
    rows = left.shape[0]
    return three(out[:rows, :LANES] + out[rows:, :LANES] + out[:rows, LANES:])


def norm_weights(t, part, m_ref, out_ref):
    pieces = []
    for g in range(2):
        start = 512 * g
        x = m_ref[t, :, part * WIDTH + start : part * WIDTH + start + WIDE]
        col = lax.broadcasted_iota(jnp.int32, (8, WIDE), 1) + start
        head = lax.broadcasted_iota(jnp.int32, (8, WIDE), 0) + 8 * g
        inside = (col >= HD * head) & (col < HD * (head + 1))
        left = [jnp.where(inside, x[e : e + 1], 0.0) for e in range(TERMS)]
        out = product(jnp.concatenate(left, axis=0), x * (1.0 / HD))
        pieces.append(out.reshape(TERMS, 8, LANES))
    both = jnp.concatenate(pieces, axis=1)
    out_ref[t] = both.reshape(TERMS * HEADS, LANES).astype(bf16)


def fold_scores(t, m_ref, gain_ref, at_ref, bk_ref, bq_ref):
    norm_weights(t, 0, m_ref, bq_ref)
    norm_weights(t, 1, m_ref, bk_ref)
    both_gains = gain_ref[0:1, :] * gain_ref[1:2, :] * (HD**-0.5 * math.log2(math.e))
    for g in range(GROUPS):
        start = 256 * g
        mq = m_ref[t, :, start : start + WINDOW_LANES]
        mk = m_ref[t, :, WIDTH + start : WIDTH + start + WINDOW_LANES]
        mk = mk * both_gains[:, start : start + WINDOW_LANES]
        col = lax.broadcasted_iota(jnp.int32, (FE, WINDOW_LANES), 1) + start
        left = []
        for p in range(4):
            h = 4 * g + p
            left.append(jnp.where((col >= HD * h) & (col < HD * (h + 1)), mk, 0.0))
        a = product(jnp.concatenate(left, axis=0), mq)
        for p in range(4):
            piece = a[FE * p : FE * (p + 1)]
            full = jnp.concatenate(
                [piece, piece, piece, jnp.zeros((LANES - 3 * FE, LANES), f32)], axis=0
            )
            at_ref[t, pl.ds(LANES * (4 * g + p), LANES), :] = full.astype(bf16)


def fold_values(t, m_ref, mv_ref):
    for g in range(2):
        start = 512 * g
        mv = m_ref[t, :, 2 * WIDTH + start : 2 * WIDTH + start + WIDE]
        mv = jnp.concatenate([mv, jnp.zeros((32 - FE, WIDE), f32)], axis=0)
        col = lax.broadcasted_iota(jnp.int32, (32, WIDE), 1) + start
        for p in range(8):
            h = 8 * g + p
            inside = (col >= HD * h) & (col < HD * (h + 1))
            mv_ref[t, g, pl.ds(32 * p, 32), :] = jnp.where(inside, mv, 0.0).astype(bf16)


def features_of(x, gram):
    g = dot(gram, x.astype(bf16))
    t = g[:PATCH] + g[PATCH : 2 * PATCH] + g[2 * PATCH :]
    spread = jnp.sum(x * t, axis=0, keepdims=True)
    u = x * lax.rsqrt(jnp.maximum(spread, 0.0) + norm_eps)
    count = x.shape[1]
    first = lax.broadcasted_iota(jnp.int32, (FE - PATCH, count), 0) == 0
    u = jnp.concatenate([u, jnp.where(first, 1.0, 0.0)], axis=0)
    high = u.astype(bf16).astype(f32)
    low = u - high
    f = jnp.concatenate([high, high, low, jnp.zeros((LANES - 3 * FE, count), f32)], axis=0)
    return u, f.astype(bf16)


def head_scale(weights, u, f):
    t = dot(weights, f)
    total = t[:HEADS] * u[:1]
    for e in range(1, TERMS):
        total = total + t[HEADS * e : HEADS * (e + 1)] * u[e : e + 1]
    return lax.rsqrt(jnp.maximum(total, 0.0) + norm_eps)


def own_queries(sweep, own, gram, at_ref, bq_ref, qs):
    row = lax.broadcasted_iota(jnp.int32, (LANES, LANES), 0)
    left = lax.broadcasted_iota(jnp.int32, (1, LANES), 1) < OWN
    t = STEPS_DEV * sweep
    u, f = features_of(own.astype(f32), gram)
    scale = jnp.where(left, head_scale(bq_ref[t], u, f), head_scale(bq_ref[t + 1], u, f))
    for h in range(HEADS):
        lines = pl.ds(LANES * h, LANES)
        q = jnp.where(left, dot(at_ref[t, lines, :], f), dot(at_ref[t + 1, lines, :], f))
        q = q * scale[h : h + 1]
        high = q.astype(bf16).astype(f32)
        q = jnp.where((row >= FE) & (row < 2 * FE), q - high, high).T.astype(bf16)
        for s in range(STEPS_DEV):
            qs[s, h // HB, pl.ds(OWN * (h % HB), OWN), :] = q[OWN * s : OWN * (s + 1)]


def halves(all_ref, xs):
    left = lax.broadcasted_iota(jnp.int32, (PATCH, LANES), 1) < OWN
    for p in range(all_ref.shape[0] // 2):
        a = all_ref[2 * p].astype(f32)
        b = all_ref[2 * p + 1].astype(f32)
        cols = pl.ds(LANES * p, LANES)
        xs[0, :, cols] = jnp.where(left, a, pltpu.roll(b, OWN, 1))
        xs[1, :, cols] = jnp.where(left, pltpu.roll(a, OWN, 1), b)


def keys_of(x_ref, gram, kf, scales):
    for n in range(x_ref.shape[1] // CHUNK):
        cols = pl.ds(n * CHUNK, CHUNK)
        u, f = features_of(x_ref[:, cols], gram)
        kf[:, cols] = f
        for weights, rho in scales:
            scale = head_scale(weights, u, f)
            for g in range(GROUPS):
                rho[g, pl.ds(0, 4), cols] = scale[4 * g : 4 * g + 4]


def stages(score, soft, value, tokens):
    lane = lax.broadcasted_iota(jnp.int32, (OWN, LANES), 1)
    parts = tokens // 256
    if value is not None:
        out = jnp.zeros((ROWS, LANES), f32)
    for n in range(parts):
        keys = pl.ds(256 * n, 256)
        if score is not None:
            t = dot(score["q"][...], score["kf"][:, keys])
            for p in range(HB):
                r = score["rho"][score["part"] * (HB // 4) + p // 4, pl.ds(p % 4, 1), keys]
                score["sc"][pl.ds(OWN * p, OWN), keys] = t[OWN * p : OWN * (p + 1)] * r
        if soft is not None:
            some = ROWS // parts
            for m in range(some // SUB):
                lines = pl.ds(some * n + SUB * m, SUB)
                x = soft["sc"][lines, :]
                x = x - jnp.max(x, axis=1, keepdims=True)
                soft["pr"][lines, :] = jnp.exp2(x).astype(bf16)
        if value is not None:
            out = out + dot_nt(value["pr"][:, keys], value["kf"][:, keys])
    if value is not None:
        o = out + pltpu.roll(out, LANES - 2 * FE, 1)
        for g in range(HB // 4):
            z = jnp.zeros((OWN, LANES), f32)
            for p in range(4):
                at = OWN * (4 * g + p)
                piece = o[at : at + OWN]
                piece = jnp.where(lane < FE, piece / piece[:, PATCH : PATCH + 1], 0.0)
                z = z + (pltpu.roll(piece, 32 * p, 1) if p else piece)
            value["zs"][value["part"] * (HB // 4) + g] = z.astype(bf16)


def velocity_terms(sweep, sizes, own_ref, zs, mv_ref, w_o, w_in, w_out_t, out_ref):
    attended = []
    for s in range(STEPS_DEV):
        t = STEPS_DEV * sweep + s
        a = dot(jnp.concatenate([zs[s, 0], zs[s, 1]], axis=1), mv_ref[t, 0])
        b = dot(jnp.concatenate([zs[s, 2], zs[s, 3]], axis=1), mv_ref[t, 1])
        a = [a[:, :512], a[:, 512:] + b[:, :LANES], b[:, LANES:]]
        attended.append(jnp.concatenate(a, axis=1).astype(bf16))
    embedded = lax.dot_general(
        own_ref[...], w_in[...], (((0,), (0,)), ((), ())), preferred_element_type=f32
    )
    mixed = embedded + dot(jnp.concatenate(attended, axis=0), w_o[...])
    centered = mixed - jnp.mean(mixed, axis=1, keepdims=True)
    spread = jnp.mean(centered * centered, axis=1, keepdims=True)
    normed = (centered * lax.rsqrt(spread + norm_eps)).astype(bf16)
    left = lax.broadcasted_iota(jnp.int32, (1, LANES), 1) < OWN
    out_ref[...] = dot_nt(w_out_t[...], normed) * jnp.where(left, sizes[0], sizes[1])


class Exchange:
    def __init__(self, axis, count, src, dst, send, recv):
        self.axis, self.count, self.src, self.dst = axis, count, src, dst
        self.send, self.recv = send, recv
        self.me = lax.axis_index(axis)

    def start(self):
        @pl.loop(1, self.count)
        def _(i):
            pltpu.make_async_remote_copy(
                src_ref=self.src,
                dst_ref=self.dst.at[self.me],
                send_sem=self.send,
                recv_sem=self.recv,
                device_id={self.axis: lax.rem(self.me + i, self.count)},
                device_id_type=MESH,
            ).start()

        self.dst[self.me] = self.src[...]

    def wait(self):
        others = self.dst.at[pl.ds(0, self.count - 1)]
        pltpu.make_async_copy(others, others, self.recv).wait()
        pltpu.make_async_copy(others, others, self.send).wait()


def greet(barrier, axis, count):
    me = lax.axis_index(axis)

    @pl.loop(1, count)
    def _(i):
        pl.semaphore_signal(
            barrier, inc=1, device_id={axis: lax.rem(me + i, count)}, device_id_type=MESH
        )


def picard(shift, anchor, terms_ref):
    half = lax.broadcasted_iota(jnp.int32, (1, LANES), 1) // OWN
    first = STEPS_DEV * lax.axis_index("slab") + shift
    state, new_anchor = anchor, anchor
    for k in range(terms_ref.shape[0]):
        term = terms_ref[k]
        turned = pltpu.roll(term, OWN, 1)
        here, there = STEPS_DEV * k + half, STEPS_DEV * k + 1 - half
        state = state + jnp.where(here < first + half, term, 0.0)
        state = state + jnp.where(there < first + half, turned, 0.0)
        new_anchor = new_anchor + jnp.where(here < shift, term, 0.0)
        new_anchor = new_anchor + jnp.where(there < shift, turned, 0.0)
    return state, new_anchor


def window_kernel(
    plan_ref, slides_ref, freq_ref, noise_ref, w_in_hbm, w_mod_hbm, w_qkv_hbm, gain_hbm, w_o_hbm,
    w_out_hbm, moved_ref,
    noise, w_in, w_mod, wq, wk, wv, gain, w_o, w_out_t, load,
    lhs, m_ref, gram, at_ref, bk_ref, bq_ref, mv_ref,
    anchor, moved, packed, own0, own1, all0, all1, terms, every,
    send0, recv0, send1, recv1, send2, recv2,
    xs, kf0, kf1, rho, qs, sc0, sc1, pr0, pr1, zs,
):
    slabs, count = every.shape[2], all0.shape[0]
    tokens = count * OWN
    columns = [w_qkv_hbm.at[:, pl.ds(WIDTH * n, WIDTH)] for n in range(3)]
    pairs = (
        (noise_ref, noise), (w_in_hbm, w_in), (w_mod_hbm, w_mod), (columns[0], wq),
        (columns[1], wk), (gain_hbm, gain), (columns[2], wv), (w_out_hbm, w_out_t),
        (w_o_hbm, w_o),
    )
    loads = [pltpu.make_async_copy(a, b, load.at[n]) for n, (a, b) in enumerate(pairs)]
    for copy in loads:
        copy.start()
    barrier = pltpu.get_barrier_semaphore()
    greet(barrier, "seq", count)
    greet(barrier, "slab", slabs)

    loads[0].wait()
    packed[...] = jnp.concatenate([noise[0], noise[1]], axis=1).astype(bf16)
    for c in range(CLIPS):
        anchor[c] = jnp.concatenate([noise[c], noise[c]], axis=1)
        moved[c] = jnp.zeros_like(anchor[c])
        own0[c] = anchor[c].astype(bf16)
    pl.semaphore_wait(barrier, count + slabs - 2)
    gather0 = Exchange("seq", count, packed, all0, send0.at[0], recv0.at[0])
    gather0.start()
    loads[1].wait()
    loads[2].wait()
    modulated_rows(plan_ref, slides_ref, freq_ref, w_mod, w_in, gram, lhs)
    for n, part in enumerate((wq, wk)):
        loads[3 + n].wait()
        project(lhs, part, m_ref, n)
    loads[5].wait()
    for t in range(STEPS_DEV):
        fold_scores(t, m_ref, gain, at_ref, bk_ref, bq_ref)

    square = gram[...]
    own = (own0, own1)
    per = HEADS // HB
    gathers = [
        Exchange("seq", count, own1.at[c], all1.at[c], send2.at[c], recv2.at[c])
        for c in range(CLIPS)
    ]
    sums = [
        [
            Exchange(
                "slab", slabs, terms.at[w, c], every.at[w, c], send1.at[w, c], recv1.at[w, c]
            )
            for c in range(CLIPS)
        ]
        for w in range(SWEEPS)
    ]

    def queries(w, c):
        own_queries(w, own[w][c], square, at_ref, bq_ref, qs.at[c])

    def finish(w, c):
        first = STEPS_DEV * lax.axis_index("slab")
        if w:
            first = first + slides_ref[0]
        levels = [plan_ref[first + a].astype(f32) for a in range(STEPS_DEV + 1)]
        sizes = [(levels[a + 1] - levels[a]) / 1000.0 for a in range(STEPS_DEV)]
        velocity_terms(
            w, sizes, own[w].at[c], zs.at[c], mv_ref, w_o, w_in, w_out_t, terms.at[w, c]
        )

    def send(w, c):
        sums[w][c].start()

    def slide(w, c):
        sums[w][c].wait()
        return picard(slides_ref[w], moved[c], every.at[w, c])

    def advance(c):
        state, moved[c] = slide(0, c)
        own1[c] = (anchor[c] + state).astype(bf16)
        gathers[c].start()

    def receive(c):
        gathers[c].wait()
        halves(all1.at[c], xs)
        for s in range(STEPS_DEV):
            scales = [(bk_ref[STEPS_DEV + s], rho.at[c, s])]
            keys_of(xs.at[s], square, kf1.at[c, s], scales)

    blocks = []
    for w in range(SWEEPS):
        for c in range(CLIPS):
            for s in range(STEPS_DEV):
                for part in range(per):
                    slot = len(blocks) % 2
                    blocks.append(
                        dict(
                            q=qs.at[c, s, part], kf=kf1.at[c, s] if w else kf0.at[c],
                            rho=rho.at[c, s], part=part, sc=(sc0, sc1)[slot],
                            pr=(pr0, pr1)[slot], zs=zs.at[c, s],
                        )
                    )
    one = STEPS_DEV * per
    turn = CLIPS * one

    def stage(n, low, high):
        def pick(k):
            return blocks[k] if low <= k < high else None

        stages(pick(n), pick(n - 1), pick(n - 2), tokens)

    for c in range(CLIPS):
        queries(0, c)
    loads[6].wait()
    project(lhs, wv, m_ref, 2)
    for t in range(STEPS_DEV):
        fold_values(t, m_ref, mv_ref)
    loads[7].wait()
    loads[8].wait()
    gather0.wait()
    halves(all0, xs)
    for c in range(CLIPS):
        scales = [(bk_ref[s], rho.at[c, s]) for s in range(STEPS_DEV)]
        keys_of(xs.at[c], square, kf0.at[c], scales)
    for n in range(turn + 2):
        stage(n, 0, turn)
        if n == one + 1:
            finish(0, 0)
            send(0, 0)
        if n == turn:
            advance(0)
    finish(0, 1)
    send(0, 1)

    @pl.loop(STEPS_DEV, COMBOS)
    def _(t):
        fold_scores(t, m_ref, gain, at_ref, bk_ref, bq_ref)
        fold_values(t, m_ref, mv_ref)

    queries(1, 0)
    advance(1)
    receive(0)
    for n in range(turn, 2 * turn + 2):
        if n == turn + one:
            queries(1, 1)
            receive(1)
        stage(n, turn, 2 * turn)
        if n == turn + one + 1:
            finish(1, 0)
        if n == turn + one + 2:
            send(1, 0)
    finish(1, 1)
    send(1, 1)
    for c in range(CLIPS):
        state, last = slide(1, c)
        for s in range(STEPS_DEV):
            moved_ref[s, c] = state[:, OWN * s : OWN * (s + 1)]
        moved_ref[STEPS_DEV, c] = last[:, :OWN]


def add_kernel(noise_ref, moved_ref, states_ref, anchor_ref):
    for s in range(STEPS_DEV):
        states_ref[s] = noise_ref[...] + moved_ref[s]
    anchor_ref[...] = noise_ref[...] + moved_ref[STEPS_DEV]


def on_device(noise, plan, slides, w_in, w_mod, w_qkv, qk_gain, w_o, w_out):
    slabs, count = lax.axis_size("slab"), lax.axis_size("seq")
    tokens = count * OWN
    half = FREQ // 2
    freq = np.exp(-math.log(10000.0) * np.arange(half) / half).astype(np.float32)[None]
    smem = pl.BlockSpec(memory_space=pltpu.SMEM)
    vmem = pl.BlockSpec(memory_space=pltpu.VMEM)
    far = pl.BlockSpec(memory_space=pl.ANY)
    block = (PATCH, LANES)

    def sems(*shape):
        return [pltpu.SemaphoreType.DMA(shape), pltpu.SemaphoreType.DMA(shape)]

    moved = pl.pallas_call(
        window_kernel,
        in_specs=[smem, smem, vmem] + [far] * 7,
        out_specs=vmem,
        out_shape=jax.ShapeDtypeStruct((STEPS_DEV + 1, CLIPS, PATCH, OWN), f32),
        scratch_shapes=[
            pltpu.VMEM((CLIPS, PATCH, OWN), f32),
            pltpu.VMEM((PATCH, WIDTH), bf16),
            pltpu.VMEM((FREQ, 2 * WIDTH), bf16),
            pltpu.VMEM((WIDTH, WIDTH), bf16),
            pltpu.VMEM((WIDTH, WIDTH), bf16),
            pltpu.VMEM((WIDTH, WIDTH), bf16),
            pltpu.VMEM((2, WIDTH), f32),
            pltpu.VMEM((WIDTH, WIDTH), bf16),
            pltpu.VMEM((PATCH, WIDTH), bf16),
            pltpu.SemaphoreType.DMA((9,)),
            pltpu.VMEM((2 * COMBOS * FE, WIDTH), bf16),
            pltpu.VMEM((COMBOS, FE, 3 * WIDTH), f32),
            pltpu.VMEM((3 * PATCH, PATCH), bf16),
            pltpu.VMEM((COMBOS, HEADS * LANES, LANES), bf16),
            pltpu.VMEM((COMBOS, HEADS * TERMS, LANES), bf16),
            pltpu.VMEM((COMBOS, HEADS * TERMS, LANES), bf16),
            pltpu.VMEM((COMBOS, 2, HEADS * 16, WIDE), bf16),
            pltpu.VMEM((CLIPS,) + block, f32),
            pltpu.VMEM((CLIPS,) + block, f32),
            pltpu.VMEM(block, bf16),
            pltpu.VMEM((CLIPS,) + block, bf16),
            pltpu.VMEM((CLIPS,) + block, bf16),
            pltpu.VMEM((count,) + block, bf16),
            pltpu.VMEM((CLIPS, count) + block, bf16),
            pltpu.VMEM((SWEEPS, CLIPS) + block, f32),
            pltpu.VMEM((SWEEPS, CLIPS, slabs) + block, f32),
            *sems(1), *sems(SWEEPS, CLIPS), *sems(CLIPS),
            pltpu.VMEM((2, PATCH, tokens), f32),
            pltpu.VMEM((CLIPS, LANES, tokens), bf16),
            pltpu.VMEM((CLIPS, STEPS_DEV, LANES, tokens), bf16),
            pltpu.VMEM((CLIPS, STEPS_DEV, GROUPS, 8, tokens), f32),
            pltpu.VMEM((CLIPS, STEPS_DEV, HEADS // HB, ROWS, LANES), bf16),
            pltpu.VMEM((ROWS, tokens), f32),
            pltpu.VMEM((ROWS, tokens), f32),
            pltpu.VMEM((ROWS, tokens), bf16),
            pltpu.VMEM((ROWS, tokens), bf16),
            pltpu.VMEM((CLIPS, STEPS_DEV, GROUPS, OWN, LANES), bf16),
        ],
        compiler_params=pltpu.CompilerParams(
            collective_id=1, has_side_effects=True, vmem_limit_bytes=56 << 20
        ),
    )(plan, slides, freq, noise, w_in, w_mod, w_qkv, qk_gain, w_o, w_out.T)
    return pl.pallas_call(
        add_kernel,
        in_specs=[vmem, vmem],
        out_specs=[vmem, vmem],
        out_shape=[
            jax.ShapeDtypeStruct((STEPS_DEV, CLIPS, PATCH, OWN), f32),
            jax.ShapeDtypeStruct((CLIPS, PATCH, OWN), f32),
        ],
    )(noise, moved)


def solution(mesh):
    return jax.shard_map(
        on_device,
        mesh=mesh,
        in_specs=(P(None, None, "seq"), P(), P(), P(), P(), P(), P(), P(), P()),
        out_specs=(P("slab", None, None, "seq"), P(None, None, "seq")),
        check_vma=False,
    )
```

```python
import math

import jax
import jax.numpy as jnp
import numpy as np
from jax import lax
from jax.experimental import pallas as pl
from jax.experimental.pallas import tpu as pltpu
from jax.sharding import PartitionSpec as P

HEADS = 16
HD = 72
STEPS_DEV = 2
SWEEPS = 2
COMBOS = STEPS_DEV * SWEEPS
CLIPS = 2
PATCH = 16
FREQ = 256
FE = 24
LANES = 128
OWN = 64
WIDTH = HEADS * HD
GROUPS = 4
WINDOW_LANES = 384
WIDE = 640
TERMS = PATCH + 1
HB = 8
ROWS = HB * OWN
CHUNK = 1024

norm_eps = 1e-06
MESH = pl.DeviceIdType.MESH
f32 = jnp.float32
bf16 = jnp.bfloat16


def dot(a, b):
    return lax.dot_general(a, b, (((1,), (0,)), ((), ())), preferred_element_type=f32)


def dot_nt(a, b):
    return lax.dot_general(a, b, (((1,), (1,)), ((), ())), preferred_element_type=f32)


def split(x):
    high = x.astype(bf16)
    return high, (x - high.astype(f32)).astype(bf16)


def modulated_rows(plan_ref, slides_ref, freq_ref, w_mod, w_in, gram, lhs):
    first = STEPS_DEV * lax.axis_index("slab")
    row = lax.broadcasted_iota(jnp.int32, (8, FREQ // 2), 0)
    level = jnp.zeros((8, FREQ // 2), f32)
    for t in range(COMBOS):
        place = first + t % STEPS_DEV
        if t >= STEPS_DEV:
            place = place + slides_ref[0]
        level = jnp.where(row == t, plan_ref[place].astype(f32), level)
    angles = level * freq_ref[...]
    features = jnp.concatenate([jnp.cos(angles), jnp.sin(angles)], axis=1).astype(bf16)
    modulation = dot(features, w_mod[...])
    wide = w_in[...].astype(f32)
    centered = wide - jnp.mean(wide, axis=1, keepdims=True)
    square = lax.dot_general(
        centered, centered, (((1,), (1,)), ((), ())),
        precision=lax.Precision.HIGHEST, preferred_element_type=f32,
    ) * (1.0 / WIDTH)
    g1 = square.astype(bf16)
    rest = square - g1.astype(f32)
    g2 = rest.astype(bf16)
    g3 = (rest - g2.astype(f32)).astype(bf16)
    for n, g in enumerate((g1, g2, g3)):
        gram[pl.ds(PATCH * n, PATCH), :] = g
    under = lax.broadcasted_iota(jnp.int32, (FE - PATCH, WIDTH), 0)
    rows = []
    for t in range(COMBOS):
        rows.append(centered * (1.0 + modulation[t : t + 1, :WIDTH]))
        rows.append(jnp.where(under == 0, modulation[t : t + 1, WIDTH:], 0.0))
    high, low = split(jnp.concatenate(rows, axis=0))
    lhs[pl.ds(0, COMBOS * FE), :] = high
    lhs[pl.ds(COMBOS * FE, COMBOS * FE), :] = low


def project(lhs, w_part, m_ref, part):
    @pl.loop(0, WIDTH // WINDOW_LANES)
    def _(n):
        at = pl.multiple_of(n * WINDOW_LANES, WINDOW_LANES)
        both = dot(lhs[...], w_part[:, pl.ds(at, WINDOW_LANES)])
        both = both[: COMBOS * FE] + both[COMBOS * FE :]
        to = pl.ds(pl.multiple_of(part * WIDTH + at, LANES), WINDOW_LANES)
        for t in range(COMBOS):
            m_ref[t, :, to] = both[FE * t : FE * (t + 1)]


def three(x):
    high = x.astype(bf16).astype(f32)
    col = lax.broadcasted_iota(jnp.int32, x.shape, 1)
    return jnp.where((col >= FE) & (col < 2 * FE), x - high, high)


def product(left, right):
    pad = jnp.zeros((LANES - 3 * FE, right.shape[1]), f32)
    right = jnp.concatenate([right, right, right, pad], axis=0)
    high, top = left.astype(bf16).astype(f32), right.astype(bf16).astype(f32)
    out = dot_nt(
        jnp.concatenate([high, left - high], axis=0).astype(bf16),
        jnp.concatenate([top, right - top], axis=0).astype(bf16),
    )
    rows = left.shape[0]
    return three(out[:rows, :LANES] + out[rows:, :LANES] + out[:rows, LANES:])


def norm_weights(t, part, m_ref, out_ref):
    pieces = []
    for g in range(2):
        start = 512 * g
        x = m_ref[t, :, part * WIDTH + start : part * WIDTH + start + WIDE]
        col = lax.broadcasted_iota(jnp.int32, (8, WIDE), 1) + start
        head = lax.broadcasted_iota(jnp.int32, (8, WIDE), 0) + 8 * g
        inside = (col >= HD * head) & (col < HD * (head + 1))
        left = [jnp.where(inside, x[e : e + 1], 0.0) for e in range(TERMS)]
        out = product(jnp.concatenate(left, axis=0), x * (1.0 / HD))
        pieces.append(out.reshape(TERMS, 8, LANES))
    both = jnp.concatenate(pieces, axis=1)
    out_ref[t] = both.reshape(TERMS * HEADS, LANES).astype(bf16)


def fold_scores(t, m_ref, gain_ref, at_ref, bk_ref, bq_ref):
    norm_weights(t, 0, m_ref, bq_ref)
    norm_weights(t, 1, m_ref, bk_ref)
    both_gains = gain_ref[0:1, :] * gain_ref[1:2, :] * (HD**-0.5 * math.log2(math.e))
    for g in range(GROUPS):
        start = 256 * g
        mq = m_ref[t, :, start : start + WINDOW_LANES]
        mk = m_ref[t, :, WIDTH + start : WIDTH + start + WINDOW_LANES]
        mk = mk * both_gains[:, start : start + WINDOW_LANES]
        col = lax.broadcasted_iota(jnp.int32, (FE, WINDOW_LANES), 1) + start
        left = []
        for p in range(4):
            h = 4 * g + p
            left.append(jnp.where((col >= HD * h) & (col < HD * (h + 1)), mk, 0.0))
        a = product(jnp.concatenate(left, axis=0), mq)
        for p in range(4):
            piece = a[FE * p : FE * (p + 1)]
            full = jnp.concatenate(
                [piece, piece, piece, jnp.zeros((LANES - 3 * FE, LANES), f32)], axis=0
            )
            at_ref[t, pl.ds(LANES * (4 * g + p), LANES), :] = full.astype(bf16)


def fold_values(t, m_ref, mv_ref):
    for g in range(2):
        start = 512 * g
        mv = m_ref[t, :, 2 * WIDTH + start : 2 * WIDTH + start + WIDE]
        mv = jnp.concatenate([mv, jnp.zeros((32 - FE, WIDE), f32)], axis=0)
        col = lax.broadcasted_iota(jnp.int32, (32, WIDE), 1) + start
        for p in range(8):
            h = 8 * g + p
            inside = (col >= HD * h) & (col < HD * (h + 1))
            mv_ref[t, g, pl.ds(32 * p, 32), :] = jnp.where(inside, mv, 0.0).astype(bf16)


def features_of(x, gram):
    g = dot(gram, x.astype(bf16))
    t = g[:PATCH] + g[PATCH : 2 * PATCH] + g[2 * PATCH :]
    spread = jnp.sum(x * t, axis=0, keepdims=True)
    u = x * lax.rsqrt(jnp.maximum(spread, 0.0) + norm_eps)
    count = x.shape[1]
    first = lax.broadcasted_iota(jnp.int32, (FE - PATCH, count), 0) == 0
    u = jnp.concatenate([u, jnp.where(first, 1.0, 0.0)], axis=0)
    high = u.astype(bf16).astype(f32)
    low = u - high
    f = jnp.concatenate([high, high, low, jnp.zeros((LANES - 3 * FE, count), f32)], axis=0)
    return u, f.astype(bf16)


def head_scale(weights, u, f):
    t = dot(weights, f)
    total = t[:HEADS] * u[:1]
    for e in range(1, TERMS):
        total = total + t[HEADS * e : HEADS * (e + 1)] * u[e : e + 1]
    return lax.rsqrt(jnp.maximum(total, 0.0) + norm_eps)


def own_queries(sweep, own, gram, at_ref, bq_ref, qs):
    row = lax.broadcasted_iota(jnp.int32, (LANES, LANES), 0)
    left = lax.broadcasted_iota(jnp.int32, (1, LANES), 1) < OWN
    t = STEPS_DEV * sweep
    u, f = features_of(own.astype(f32), gram)
    scale = jnp.where(left, head_scale(bq_ref[t], u, f), head_scale(bq_ref[t + 1], u, f))
    for h in range(HEADS):
        lines = pl.ds(LANES * h, LANES)
        q = jnp.where(left, dot(at_ref[t, lines, :], f), dot(at_ref[t + 1, lines, :], f))
        q = q * scale[h : h + 1]
        high = q.astype(bf16).astype(f32)
        q = jnp.where((row >= FE) & (row < 2 * FE), q - high, high).T.astype(bf16)
        for s in range(STEPS_DEV):
            qs[s, h // HB, pl.ds(OWN * (h % HB), OWN), :] = q[OWN * s : OWN * (s + 1)]


def halves(all_ref, xs):
    left = lax.broadcasted_iota(jnp.int32, (PATCH, LANES), 1) < OWN
    for p in range(all_ref.shape[0] // 2):
        a = all_ref[2 * p].astype(f32)
        b = all_ref[2 * p + 1].astype(f32)
        cols = pl.ds(LANES * p, LANES)
        xs[0, :, cols] = jnp.where(left, a, pltpu.roll(b, OWN, 1))
        xs[1, :, cols] = jnp.where(left, pltpu.roll(a, OWN, 1), b)


def keys_of(x_ref, gram, kf, scales):
    for n in range(x_ref.shape[1] // CHUNK):
        cols = pl.ds(n * CHUNK, CHUNK)
        u, f = features_of(x_ref[:, cols], gram)
        kf[:, cols] = f
        for weights, rho in scales:
            scale = head_scale(weights, u, f)
            for g in range(GROUPS):
                rho[g, pl.ds(0, 4), cols] = scale[4 * g : 4 * g + 4]


def stages(score, soft, value, tokens):
    lane = lax.broadcasted_iota(jnp.int32, (OWN, LANES), 1)
    parts = tokens // 256
    if value is not None:
        out = jnp.zeros((ROWS, LANES), f32)
    for n in range(parts):
        keys = pl.ds(256 * n, 256)
        if score is not None:
            t = dot(score["q"][...], score["kf"][:, keys])
            for p in range(HB):
                r = score["rho"][score["part"] * (HB // 4) + p // 4, pl.ds(p % 4, 1), keys]
                lines = pl.ds(OWN * p, OWN)
                x = t[OWN * p : OWN * (p + 1)] * r
                score["sc"][lines, keys] = x
                top = jnp.maximum(x[:, :LANES], x[:, LANES:])
                if n:
                    top = jnp.maximum(score["top"][lines, :], top)
                score["top"][lines, :] = top
        if soft is not None:
            some = ROWS // parts
            lines = pl.ds(some * n, some)
            top = jnp.max(soft["top"][lines, :], axis=1, keepdims=True)
            top = jnp.broadcast_to(top, (some, LANES))
            for m in range(tokens // LANES):
                cols = pl.ds(LANES * m, LANES)
                soft["pr"][lines, cols] = jnp.exp2(soft["sc"][lines, cols] - top).astype(bf16)
        if value is not None:
            out = out + dot_nt(value["pr"][:, keys], value["kf"][:, keys])
    if value is not None:
        o = out + pltpu.roll(out, LANES - 2 * FE, 1)
        for g in range(HB // 4):
            z = jnp.zeros((OWN, LANES), f32)
            for p in range(4):
                at = OWN * (4 * g + p)
                piece = o[at : at + OWN]
                piece = jnp.where(lane < FE, piece / piece[:, PATCH : PATCH + 1], 0.0)
                z = z + (pltpu.roll(piece, 32 * p, 1) if p else piece)
            value["zs"][value["part"] * (HB // 4) + g] = z.astype(bf16)


def velocity_terms(sweep, sizes, own_ref, zs, mv_ref, w_o, w_in, w_out_t, out_ref):
    attended = []
    for s in range(STEPS_DEV):
        t = STEPS_DEV * sweep + s
        a = dot(jnp.concatenate([zs[s, 0], zs[s, 1]], axis=1), mv_ref[t, 0])
        b = dot(jnp.concatenate([zs[s, 2], zs[s, 3]], axis=1), mv_ref[t, 1])
        a = [a[:, :512], a[:, 512:] + b[:, :LANES], b[:, LANES:]]
        attended.append(jnp.concatenate(a, axis=1).astype(bf16))
    embedded = lax.dot_general(
        own_ref[...], w_in[...], (((0,), (0,)), ((), ())), preferred_element_type=f32
    )
    mixed = embedded + dot(jnp.concatenate(attended, axis=0), w_o[...])
    centered = mixed - jnp.mean(mixed, axis=1, keepdims=True)
    spread = jnp.mean(centered * centered, axis=1, keepdims=True)
    normed = (centered * lax.rsqrt(spread + norm_eps)).astype(bf16)
    left = lax.broadcasted_iota(jnp.int32, (1, LANES), 1) < OWN
    out_ref[...] = dot_nt(w_out_t[...], normed) * jnp.where(left, sizes[0], sizes[1])


class Exchange:
    def __init__(self, axis, count, src, dst, send, recv):
        self.axis, self.count, self.src, self.dst = axis, count, src, dst
        self.send, self.recv = send, recv
        self.me = lax.axis_index(axis)

    def start(self):
        @pl.loop(1, self.count)
        def _(i):
            pltpu.make_async_remote_copy(
                src_ref=self.src,
                dst_ref=self.dst.at[self.me],
                send_sem=self.send,
                recv_sem=self.recv,
                device_id={self.axis: lax.rem(self.me + i, self.count)},
                device_id_type=MESH,
            ).start()

        self.dst[self.me] = self.src[...]

    def wait(self):
        others = self.dst.at[pl.ds(0, self.count - 1)]
        pltpu.make_async_copy(others, others, self.recv).wait()
        pltpu.make_async_copy(others, others, self.send).wait()


def greet(barrier, axis, count):
    me = lax.axis_index(axis)

    @pl.loop(1, count)
    def _(i):
        pl.semaphore_signal(
            barrier, inc=1, device_id={axis: lax.rem(me + i, count)}, device_id_type=MESH
        )


def picard(shift, anchor, terms_ref):
    half = lax.broadcasted_iota(jnp.int32, (1, LANES), 1) // OWN
    first = STEPS_DEV * lax.axis_index("slab") + shift
    state, new_anchor = anchor, anchor
    for k in range(terms_ref.shape[0]):
        term = terms_ref[k]
        turned = pltpu.roll(term, OWN, 1)
        here, there = STEPS_DEV * k + half, STEPS_DEV * k + 1 - half
        state = state + jnp.where(here < first + half, term, 0.0)
        state = state + jnp.where(there < first + half, turned, 0.0)
        new_anchor = new_anchor + jnp.where(here < shift, term, 0.0)
        new_anchor = new_anchor + jnp.where(there < shift, turned, 0.0)
    return state, new_anchor


def window_kernel(
    plan_ref, slides_ref, freq_ref, noise_ref, w_in_hbm, w_mod_hbm, w_qkv_hbm, gain_hbm, w_o_hbm,
    w_out_hbm, moved_ref,
    noise, w_in, w_mod, wq, wk, wv, gain, w_o, w_out_t, load,
    lhs, m_ref, gram, at_ref, bk_ref, bq_ref, mv_ref,
    anchor, moved, packed, own0, own1, all0, all1, terms, every,
    send0, recv0, send1, recv1, send2, recv2,
    xs, kf0, kf1, rho, qs, sc0, sc1, pr0, pr1, top0, top1, zs,
):
    slabs, count = every.shape[2], all0.shape[0]
    tokens = count * OWN
    columns = [w_qkv_hbm.at[:, pl.ds(WIDTH * n, WIDTH)] for n in range(3)]
    pairs = (
        (noise_ref, noise), (w_in_hbm, w_in), (w_mod_hbm, w_mod), (columns[0], wq),
        (columns[1], wk), (gain_hbm, gain), (columns[2], wv), (w_out_hbm, w_out_t),
        (w_o_hbm, w_o),
    )
    loads = [pltpu.make_async_copy(a, b, load.at[n]) for n, (a, b) in enumerate(pairs)]
    for copy in loads:
        copy.start()
    barrier = pltpu.get_barrier_semaphore()
    greet(barrier, "seq", count)
    greet(barrier, "slab", slabs)

    loads[0].wait()
    packed[...] = jnp.concatenate([noise[0], noise[1]], axis=1).astype(bf16)
    for c in range(CLIPS):
        anchor[c] = jnp.concatenate([noise[c], noise[c]], axis=1)
        moved[c] = jnp.zeros_like(anchor[c])
        own0[c] = anchor[c].astype(bf16)
    pl.semaphore_wait(barrier, count + slabs - 2)
    gather0 = Exchange("seq", count, packed, all0, send0.at[0], recv0.at[0])
    gather0.start()
    loads[1].wait()
    loads[2].wait()
    modulated_rows(plan_ref, slides_ref, freq_ref, w_mod, w_in, gram, lhs)
    for n, part in enumerate((wq, wk)):
        loads[3 + n].wait()
        project(lhs, part, m_ref, n)
    loads[5].wait()
    for t in range(STEPS_DEV):
        fold_scores(t, m_ref, gain, at_ref, bk_ref, bq_ref)

    square = gram[...]
    own = (own0, own1)
    per = HEADS // HB
    gathers = [
        Exchange("seq", count, own1.at[c], all1.at[c], send2.at[c], recv2.at[c])
        for c in range(CLIPS)
    ]
    sums = [
        [
            Exchange(
                "slab", slabs, terms.at[w, c], every.at[w, c], send1.at[w, c], recv1.at[w, c]
            )
            for c in range(CLIPS)
        ]
        for w in range(SWEEPS)
    ]

    def queries(w, c):
        own_queries(w, own[w][c], square, at_ref, bq_ref, qs.at[c])

    def finish(w, c):
        first = STEPS_DEV * lax.axis_index("slab")
        if w:
            first = first + slides_ref[0]
        levels = [plan_ref[first + a].astype(f32) for a in range(STEPS_DEV + 1)]
        sizes = [(levels[a + 1] - levels[a]) / 1000.0 for a in range(STEPS_DEV)]
        velocity_terms(
            w, sizes, own[w].at[c], zs.at[c], mv_ref, w_o, w_in, w_out_t, terms.at[w, c]
        )

    def send(w, c):
        sums[w][c].start()

    def slide(w, c):
        sums[w][c].wait()
        return picard(slides_ref[w], moved[c], every.at[w, c])

    def advance(c):
        state, moved[c] = slide(0, c)
        own1[c] = (anchor[c] + state).astype(bf16)
        gathers[c].start()

    def keys0(c):
        scales = [(bk_ref[s], rho.at[c, s]) for s in range(STEPS_DEV)]
        keys_of(xs.at[c], square, kf0.at[c], scales)

    def keys1(c, s):
        scales = [(bk_ref[STEPS_DEV + s], rho.at[c, s])]
        keys_of(xs.at[s], square, kf1.at[c, s], scales)

    def receive(c):
        gathers[c].wait()
        halves(all1.at[c], xs)
        keys1(c, 0)

    blocks = []
    for w in range(SWEEPS):
        for c in range(CLIPS):
            for s in range(STEPS_DEV):
                for part in range(per):
                    slot = len(blocks) % 2
                    blocks.append(
                        dict(
                            q=qs.at[c, s, part], kf=kf1.at[c, s] if w else kf0.at[c],
                            rho=rho.at[c, s], part=part, sc=(sc0, sc1)[slot], top=(top0, top1)[slot],
                            pr=(pr0, pr1)[slot], zs=zs.at[c, s],
                        )
                    )
    one = STEPS_DEV * per
    turn = CLIPS * one

    def stage(n, low, high):
        def pick(k):
            return blocks[k] if low <= k < high else None

        stages(pick(n), pick(n - 1), pick(n - 2), tokens)

    for c in range(CLIPS):
        queries(0, c)
    loads[6].wait()
    project(lhs, wv, m_ref, 2)
    for t in range(STEPS_DEV):
        fold_values(t, m_ref, mv_ref)
    loads[7].wait()
    loads[8].wait()
    gather0.wait()
    halves(all0, xs)
    keys0(0)
    for n in range(turn + 2):
        stage(n, 0, turn)
        if n == 0:
            keys0(1)
        if n == one + 1:
            finish(0, 0)
            send(0, 0)
        if n == turn:
            advance(0)
    finish(0, 1)
    send(0, 1)

    @pl.loop(STEPS_DEV, COMBOS)
    def _(t):
        fold_scores(t, m_ref, gain, at_ref, bk_ref, bq_ref)
        fold_values(t, m_ref, mv_ref)

    queries(1, 0)
    advance(1)
    receive(0)
    for n in range(turn, 2 * turn + 2):
        if n == turn + one:
            queries(1, 1)
            receive(1)
        stage(n, turn, 2 * turn)
        if n in (turn, turn + one):
            keys1((n - turn) // one, 1)
        if n == turn + one + 1:
            finish(1, 0)
        if n == turn + one + 2:
            send(1, 0)
    finish(1, 1)
    send(1, 1)
    for c in range(CLIPS):
        state, last = slide(1, c)
        for s in range(STEPS_DEV):
            moved_ref[s, c] = state[:, OWN * s : OWN * (s + 1)]
        moved_ref[STEPS_DEV, c] = last[:, :OWN]


def add_kernel(noise_ref, moved_ref, states_ref, anchor_ref):
    for s in range(STEPS_DEV):
        states_ref[s] = noise_ref[...] + moved_ref[s]
    anchor_ref[...] = noise_ref[...] + moved_ref[STEPS_DEV]


def on_device(noise, plan, slides, w_in, w_mod, w_qkv, qk_gain, w_o, w_out):
    slabs, count = lax.axis_size("slab"), lax.axis_size("seq")
    tokens = count * OWN
    half = FREQ // 2
    freq = np.exp(-math.log(10000.0) * np.arange(half) / half).astype(np.float32)[None]
    smem = pl.BlockSpec(memory_space=pltpu.SMEM)
    vmem = pl.BlockSpec(memory_space=pltpu.VMEM)
    far = pl.BlockSpec(memory_space=pl.ANY)
    block = (PATCH, LANES)

    def sems(*shape):
        return [pltpu.SemaphoreType.DMA(shape), pltpu.SemaphoreType.DMA(shape)]

    moved = pl.pallas_call(
        window_kernel,
        in_specs=[smem, smem, vmem] + [far] * 7,
        out_specs=vmem,
        out_shape=jax.ShapeDtypeStruct((STEPS_DEV + 1, CLIPS, PATCH, OWN), f32),
        scratch_shapes=[
            pltpu.VMEM((CLIPS, PATCH, OWN), f32),
            pltpu.VMEM((PATCH, WIDTH), bf16),
            pltpu.VMEM((FREQ, 2 * WIDTH), bf16),
            pltpu.VMEM((WIDTH, WIDTH), bf16),
            pltpu.VMEM((WIDTH, WIDTH), bf16),
            pltpu.VMEM((WIDTH, WIDTH), bf16),
            pltpu.VMEM((2, WIDTH), f32),
            pltpu.VMEM((WIDTH, WIDTH), bf16),
            pltpu.VMEM((PATCH, WIDTH), bf16),
            pltpu.SemaphoreType.DMA((9,)),
            pltpu.VMEM((2 * COMBOS * FE, WIDTH), bf16),
            pltpu.VMEM((COMBOS, FE, 3 * WIDTH), f32),
            pltpu.VMEM((3 * PATCH, PATCH), bf16),
            pltpu.VMEM((COMBOS, HEADS * LANES, LANES), bf16),
            pltpu.VMEM((COMBOS, HEADS * TERMS, LANES), bf16),
            pltpu.VMEM((COMBOS, HEADS * TERMS, LANES), bf16),
            pltpu.VMEM((COMBOS, 2, HEADS * 16, WIDE), bf16),
            pltpu.VMEM((CLIPS,) + block, f32),
            pltpu.VMEM((CLIPS,) + block, f32),
            pltpu.VMEM(block, bf16),
            pltpu.VMEM((CLIPS,) + block, bf16),
            pltpu.VMEM((CLIPS,) + block, bf16),
            pltpu.VMEM((count,) + block, bf16),
            pltpu.VMEM((CLIPS, count) + block, bf16),
            pltpu.VMEM((SWEEPS, CLIPS) + block, f32),
            pltpu.VMEM((SWEEPS, CLIPS, slabs) + block, f32),
            *sems(1), *sems(SWEEPS, CLIPS), *sems(CLIPS),
            pltpu.VMEM((2, PATCH, tokens), f32),
            pltpu.VMEM((CLIPS, LANES, tokens), bf16),
            pltpu.VMEM((CLIPS, STEPS_DEV, LANES, tokens), bf16),
            pltpu.VMEM((CLIPS, STEPS_DEV, GROUPS, 8, tokens), f32),
            pltpu.VMEM((CLIPS, STEPS_DEV, HEADS // HB, ROWS, LANES), bf16),
            pltpu.VMEM((ROWS, tokens), f32),
            pltpu.VMEM((ROWS, tokens), f32),
            pltpu.VMEM((ROWS, tokens), bf16),
            pltpu.VMEM((ROWS, tokens), bf16),
            pltpu.VMEM((ROWS, LANES), f32),
            pltpu.VMEM((ROWS, LANES), f32),
            pltpu.VMEM((CLIPS, STEPS_DEV, GROUPS, OWN, LANES), bf16),
        ],
        compiler_params=pltpu.CompilerParams(
            collective_id=1, has_side_effects=True, vmem_limit_bytes=56 << 20
        ),
    )(plan, slides, freq, noise, w_in, w_mod, w_qkv, qk_gain, w_o, w_out.T)
    return pl.pallas_call(
        add_kernel,
        in_specs=[vmem, vmem],
        out_specs=[vmem, vmem],
        out_shape=[
            jax.ShapeDtypeStruct((STEPS_DEV, CLIPS, PATCH, OWN), f32),
            jax.ShapeDtypeStruct((CLIPS, PATCH, OWN), f32),
        ],
    )(noise, moved)


def solution(mesh):
    return jax.shard_map(
        on_device,
        mesh=mesh,
        in_specs=(P(None, None, "seq"), P(), P(), P(), P(), P(), P(), P(), P()),
        out_specs=(P("slab", None, None, "seq"), P(None, None, "seq")),
        check_vma=False,
    )
```

```python
import math

import jax
import jax.numpy as jnp
import numpy as np
from jax import lax
from jax.experimental import pallas as pl
from jax.experimental.pallas import tpu as pltpu
from jax.sharding import PartitionSpec as P

HEADS = 16
HD = 72
STEPS_DEV = 2
SWEEPS = 2
COMBOS = STEPS_DEV * SWEEPS
CLIPS = 2
PATCH = 16
FREQ = 256
FE = 24
LANES = 128
OWN = 64
WIDTH = HEADS * HD
GROUPS = 4
WINDOW_LANES = 384
WIDE = 640
TERMS = PATCH + 1
HB = 8
ROWS = HB * OWN
CHUNK = 1024

norm_eps = 1e-06
MESH = pl.DeviceIdType.MESH
f32 = jnp.float32
bf16 = jnp.bfloat16


def dot(a, b):
    return lax.dot_general(a, b, (((1,), (0,)), ((), ())), preferred_element_type=f32)


def dot_nt(a, b):
    return lax.dot_general(a, b, (((1,), (1,)), ((), ())), preferred_element_type=f32)


def split(x):
    high = x.astype(bf16)
    return high, (x - high.astype(f32)).astype(bf16)


def modulated_rows(plan_ref, slides_ref, freq_ref, w_mod, w_in, gram, lhs):
    first = STEPS_DEV * lax.axis_index("slab")
    row = lax.broadcasted_iota(jnp.int32, (8, FREQ // 2), 0)
    level = jnp.zeros((8, FREQ // 2), f32)
    for t in range(COMBOS):
        place = first + t % STEPS_DEV
        if t >= STEPS_DEV:
            place = place + slides_ref[0]
        level = jnp.where(row == t, plan_ref[place].astype(f32), level)
    angles = level * freq_ref[...]
    features = jnp.concatenate([jnp.cos(angles), jnp.sin(angles)], axis=1).astype(bf16)
    modulation = dot(features, w_mod[...])
    wide = w_in[...].astype(f32)
    centered = wide - jnp.mean(wide, axis=1, keepdims=True)
    square = lax.dot_general(
        centered, centered, (((1,), (1,)), ((), ())),
        precision=lax.Precision.HIGHEST, preferred_element_type=f32,
    ) * (1.0 / WIDTH)
    g1 = square.astype(bf16)
    rest = square - g1.astype(f32)
    g2 = rest.astype(bf16)
    g3 = (rest - g2.astype(f32)).astype(bf16)
    for n, g in enumerate((g1, g2, g3)):
        gram[pl.ds(PATCH * n, PATCH), :] = g
    under = lax.broadcasted_iota(jnp.int32, (FE - PATCH, WIDTH), 0)
    rows = []
    for t in range(COMBOS):
        rows.append(centered * (1.0 + modulation[t : t + 1, :WIDTH]))
        rows.append(jnp.where(under == 0, modulation[t : t + 1, WIDTH:], 0.0))
    high, low = split(jnp.concatenate(rows, axis=0))
    lhs[pl.ds(0, COMBOS * FE), :] = high
    lhs[pl.ds(COMBOS * FE, COMBOS * FE), :] = low


def project(lhs, w_part, m_ref, part):
    for n in range(WIDTH // WINDOW_LANES):
        at = n * WINDOW_LANES
        both = dot(lhs[...], w_part[:, pl.ds(at, WINDOW_LANES)])
        both = both[: COMBOS * FE] + both[COMBOS * FE :]
        to = pl.ds(part * WIDTH + at, WINDOW_LANES)
        for t in range(COMBOS):
            m_ref[t, :, to] = both[FE * t : FE * (t + 1)]


def three(x):
    high = x.astype(bf16).astype(f32)
    col = lax.broadcasted_iota(jnp.int32, x.shape, 1)
    return jnp.where((col >= FE) & (col < 2 * FE), x - high, high)


def product(left, right):
    pad = jnp.zeros((LANES - 3 * FE, right.shape[1]), f32)
    right = jnp.concatenate([right, right, right, pad], axis=0)
    high, top = left.astype(bf16).astype(f32), right.astype(bf16).astype(f32)
    out = dot_nt(
        jnp.concatenate([high, left - high], axis=0).astype(bf16),
        jnp.concatenate([top, right - top], axis=0).astype(bf16),
    )
    rows = left.shape[0]
    return three(out[:rows, :LANES] + out[rows:, :LANES] + out[:rows, LANES:])


def norm_weights(t, part, m_ref, out_ref):
    pieces = []
    for g in range(2):
        start = 512 * g
        x = m_ref[t, :, part * WIDTH + start : part * WIDTH + start + WIDE]
        col = lax.broadcasted_iota(jnp.int32, (8, WIDE), 1) + start
        head = lax.broadcasted_iota(jnp.int32, (8, WIDE), 0) + 8 * g
        inside = (col >= HD * head) & (col < HD * (head + 1))
        left = [jnp.where(inside, x[e : e + 1], 0.0) for e in range(TERMS)]
        out = product(jnp.concatenate(left, axis=0), x * (1.0 / HD))
        pieces.append(out.reshape(TERMS, 8, LANES))
    both = jnp.concatenate(pieces, axis=1)
    out_ref[t] = both.reshape(TERMS * HEADS, LANES).astype(bf16)


def fold_scores(t, m_ref, gain_ref, at_ref, bk_ref, bq_ref):
    norm_weights(t, 0, m_ref, bq_ref)
    norm_weights(t, 1, m_ref, bk_ref)
    both_gains = gain_ref[0:1, :] * gain_ref[1:2, :] * (HD**-0.5 * math.log2(math.e))
    for g in range(GROUPS):
        start = 256 * g
        mq = m_ref[t, :, start : start + WINDOW_LANES]
        mk = m_ref[t, :, WIDTH + start : WIDTH + start + WINDOW_LANES]
        mk = mk * both_gains[:, start : start + WINDOW_LANES]
        col = lax.broadcasted_iota(jnp.int32, (FE, WINDOW_LANES), 1) + start
        left = []
        for p in range(4):
            h = 4 * g + p
            left.append(jnp.where((col >= HD * h) & (col < HD * (h + 1)), mk, 0.0))
        a = product(jnp.concatenate(left, axis=0), mq)
        for p in range(4):
            piece = a[FE * p : FE * (p + 1)]
            full = jnp.concatenate(
                [piece, piece, piece, jnp.zeros((LANES - 3 * FE, LANES), f32)], axis=0
            )
            at_ref[t, pl.ds(LANES * (4 * g + p), LANES), :] = full.astype(bf16)


def fold_values(t, m_ref, mv_ref):
    for g in range(2):
        start = 512 * g
        mv = m_ref[t, :, 2 * WIDTH + start : 2 * WIDTH + start + WIDE]
        mv = jnp.concatenate([mv, jnp.zeros((32 - FE, WIDE), f32)], axis=0)
        col = lax.broadcasted_iota(jnp.int32, (32, WIDE), 1) + start
        for p in range(8):
            h = 8 * g + p
            inside = (col >= HD * h) & (col < HD * (h + 1))
            mv_ref[t, g, pl.ds(32 * p, 32), :] = jnp.where(inside, mv, 0.0).astype(bf16)


def features_of(x, gram):
    g = dot(gram, x.astype(bf16))
    t = g[:PATCH] + g[PATCH : 2 * PATCH] + g[2 * PATCH :]
    spread = jnp.sum(x * t, axis=0, keepdims=True)
    u = x * lax.rsqrt(jnp.maximum(spread, 0.0) + norm_eps)
    count = x.shape[1]
    first = lax.broadcasted_iota(jnp.int32, (FE - PATCH, count), 0) == 0
    u = jnp.concatenate([u, jnp.where(first, 1.0, 0.0)], axis=0)
    high = u.astype(bf16).astype(f32)
    low = u - high
    f = jnp.concatenate([high, high, low, jnp.zeros((LANES - 3 * FE, count), f32)], axis=0)
    return u, f.astype(bf16)


def head_scale(weights, u, f):
    t = dot(weights, f)
    total = t[:HEADS] * u[:1]
    for e in range(1, TERMS):
        total = total + t[HEADS * e : HEADS * (e + 1)] * u[e : e + 1]
    return lax.rsqrt(jnp.maximum(total, 0.0) + norm_eps)


def own_queries(sweep, own, gram, at_ref, bq_ref, qs):
    row = lax.broadcasted_iota(jnp.int32, (LANES, LANES), 0)
    left = lax.broadcasted_iota(jnp.int32, (1, LANES), 1) < OWN
    t = STEPS_DEV * sweep
    u, f = features_of(own.astype(f32), gram)
    scale = jnp.where(left, head_scale(bq_ref[t], u, f), head_scale(bq_ref[t + 1], u, f))
    for h in range(HEADS):
        lines = pl.ds(LANES * h, LANES)
        q = jnp.where(left, dot(at_ref[t, lines, :], f), dot(at_ref[t + 1, lines, :], f))
        q = q * scale[h : h + 1]
        high = q.astype(bf16).astype(f32)
        q = jnp.where((row >= FE) & (row < 2 * FE), q - high, high).T.astype(bf16)
        for s in range(STEPS_DEV):
            qs[s, h // HB, pl.ds(OWN * (h % HB), OWN), :] = q[OWN * s : OWN * (s + 1)]


def halves(all_ref, xs):
    left = lax.broadcasted_iota(jnp.int32, (PATCH, LANES), 1) < OWN
    for p in range(all_ref.shape[0] // 2):
        a = all_ref[2 * p].astype(f32)
        b = all_ref[2 * p + 1].astype(f32)
        cols = pl.ds(LANES * p, LANES)
        xs[0, :, cols] = jnp.where(left, a, pltpu.roll(b, OWN, 1))
        xs[1, :, cols] = jnp.where(left, pltpu.roll(a, OWN, 1), b)


def keys_of(x_ref, gram, kf, scales):
    for n in range(x_ref.shape[1] // CHUNK):
        cols = pl.ds(n * CHUNK, CHUNK)
        u, f = features_of(x_ref[:, cols], gram)
        kf[:, cols] = f
        for weights, rho in scales:
            scale = head_scale(weights, u, f)
            for g in range(GROUPS):
                rho[g, pl.ds(0, 4), cols] = scale[4 * g : 4 * g + 4]


def stages(score, soft, value, tokens):
    lane = lax.broadcasted_iota(jnp.int32, (OWN, LANES), 1)
    parts = tokens // 256
    if value is not None:
        out = jnp.zeros((ROWS, LANES), f32)
    for n in range(parts):
        keys = pl.ds(256 * n, 256)
        if score is not None:
            t = dot(score["q"][...], score["kf"][:, keys])
            for p in range(HB):
                r = score["rho"][score["part"] * (HB // 4) + p // 4, pl.ds(p % 4, 1), keys]
                lines = pl.ds(OWN * p, OWN)
                x = t[OWN * p : OWN * (p + 1)] * r
                score["sc"][lines, keys] = x
                top = jnp.maximum(x[:, :LANES], x[:, LANES:])
                if n:
                    top = jnp.maximum(score["top"][lines, :], top)
                score["top"][lines, :] = top
        if soft is not None:
            some = ROWS // parts
            lines = pl.ds(some * n, some)
            top = jnp.max(soft["top"][lines, :], axis=1, keepdims=True)
            top = jnp.broadcast_to(top, (some, LANES))
            for m in range(tokens // LANES):
                cols = pl.ds(LANES * m, LANES)
                soft["pr"][lines, cols] = jnp.exp2(soft["sc"][lines, cols] - top).astype(bf16)
        if value is not None:
            out = out + dot_nt(value["pr"][:, keys], value["kf"][:, keys])
    if value is not None:
        o = out + pltpu.roll(out, LANES - 2 * FE, 1)
        for g in range(HB // 4):
            z = jnp.zeros((OWN, LANES), f32)
            for p in range(4):
                at = OWN * (4 * g + p)
                piece = o[at : at + OWN]
                piece = jnp.where(lane < FE, piece / piece[:, PATCH : PATCH + 1], 0.0)
                z = z + (pltpu.roll(piece, 32 * p, 1) if p else piece)
            value["zs"][value["part"] * (HB // 4) + g] = z.astype(bf16)


def velocity_terms(sweep, sizes, own_ref, zs, mv_ref, w_o, w_in, w_out_t, out_ref):
    attended = []
    for s in range(STEPS_DEV):
        t = STEPS_DEV * sweep + s
        a = dot(jnp.concatenate([zs[s, 0], zs[s, 1]], axis=1), mv_ref[t, 0])
        b = dot(jnp.concatenate([zs[s, 2], zs[s, 3]], axis=1), mv_ref[t, 1])
        a = [a[:, :512], a[:, 512:] + b[:, :LANES], b[:, LANES:]]
        attended.append(jnp.concatenate(a, axis=1).astype(bf16))
    embedded = lax.dot_general(
        own_ref[...], w_in[...], (((0,), (0,)), ((), ())), preferred_element_type=f32
    )
    mixed = embedded + dot(jnp.concatenate(attended, axis=0), w_o[...])
    centered = mixed - jnp.mean(mixed, axis=1, keepdims=True)
    spread = jnp.mean(centered * centered, axis=1, keepdims=True)
    normed = (centered * lax.rsqrt(spread + norm_eps)).astype(bf16)
    left = lax.broadcasted_iota(jnp.int32, (1, LANES), 1) < OWN
    out_ref[...] = dot_nt(w_out_t[...], normed) * jnp.where(left, sizes[0], sizes[1])


class Exchange:
    def __init__(self, axis, count, src, dst, send, recv):
        self.axis, self.count, self.src, self.dst = axis, count, src, dst
        self.send, self.recv = send, recv
        self.me = lax.axis_index(axis)

    def start(self):
        @pl.loop(1, self.count)
        def _(i):
            pltpu.make_async_remote_copy(
                src_ref=self.src,
                dst_ref=self.dst.at[self.me],
                send_sem=self.send,
                recv_sem=self.recv,
                device_id={self.axis: lax.rem(self.me + i, self.count)},
                device_id_type=MESH,
            ).start()

        self.dst[self.me] = self.src[...]

    def wait(self):
        others = self.dst.at[pl.ds(0, self.count - 1)]
        pltpu.make_async_copy(others, others, self.recv).wait()
        pltpu.make_async_copy(others, others, self.send).wait()


def greet(barrier, axis, count):
    me = lax.axis_index(axis)

    @pl.loop(1, count)
    def _(i):
        pl.semaphore_signal(
            barrier, inc=1, device_id={axis: lax.rem(me + i, count)}, device_id_type=MESH
        )


def picard(shift, anchor, terms_ref):
    half = lax.broadcasted_iota(jnp.int32, (1, LANES), 1) // OWN
    first = STEPS_DEV * lax.axis_index("slab") + shift
    state, new_anchor = anchor, anchor
    for k in range(terms_ref.shape[0]):
        term = terms_ref[k]
        turned = pltpu.roll(term, OWN, 1)
        here, there = STEPS_DEV * k + half, STEPS_DEV * k + 1 - half
        state = state + jnp.where(here < first + half, term, 0.0)
        state = state + jnp.where(there < first + half, turned, 0.0)
        new_anchor = new_anchor + jnp.where(here < shift, term, 0.0)
        new_anchor = new_anchor + jnp.where(there < shift, turned, 0.0)
    return state, new_anchor


def window_kernel(
    plan_ref, slides_ref, freq_ref, noise_ref, w_in_hbm, w_mod_hbm, w_qkv_hbm, gain_hbm, w_o_hbm,
    w_out_hbm, moved_ref,
    noise, w_in, w_mod, wq, wk, wv, gain, w_o, w_out_t, load,
    lhs, m_ref, gram, at_ref, bk_ref, bq_ref, mv_ref,
    anchor, moved, packed, own0, own1, all0, all1, terms, every,
    send0, recv0, send1, recv1, send2, recv2,
    xs, kf0, kf1, rho, qs, sc0, sc1, pr0, pr1, top0, top1, zs,
):
    slabs, count = every.shape[2], all0.shape[0]
    tokens = count * OWN
    columns = [w_qkv_hbm.at[:, pl.ds(WIDTH * n, WIDTH)] for n in range(3)]
    pairs = (
        (noise_ref, noise), (w_in_hbm, w_in), (w_mod_hbm, w_mod), (columns[0], wq),
        (columns[1], wk), (gain_hbm, gain), (columns[2], wv), (w_out_hbm, w_out_t),
        (w_o_hbm, w_o),
    )
    loads = [pltpu.make_async_copy(a, b, load.at[n]) for n, (a, b) in enumerate(pairs)]
    for copy in loads:
        copy.start()
    barrier = pltpu.get_barrier_semaphore()
    greet(barrier, "seq", count)
    greet(barrier, "slab", slabs)

    loads[0].wait()
    packed[...] = jnp.concatenate([noise[0], noise[1]], axis=1).astype(bf16)
    for c in range(CLIPS):
        anchor[c] = jnp.concatenate([noise[c], noise[c]], axis=1)
        moved[c] = jnp.zeros_like(anchor[c])
        own0[c] = anchor[c].astype(bf16)
    pl.semaphore_wait(barrier, count + slabs - 2)
    gather0 = Exchange("seq", count, packed, all0, send0.at[0], recv0.at[0])
    gather0.start()
    loads[1].wait()
    loads[2].wait()
    modulated_rows(plan_ref, slides_ref, freq_ref, w_mod, w_in, gram, lhs)
    for n, part in enumerate((wq, wk)):
        loads[3 + n].wait()
        project(lhs, part, m_ref, n)
    loads[5].wait()
    for t in range(STEPS_DEV):
        fold_scores(t, m_ref, gain, at_ref, bk_ref, bq_ref)

    square = gram[...]
    own = (own0, own1)
    per = HEADS // HB
    gathers = [
        Exchange("seq", count, own1.at[c], all1.at[c], send2.at[c], recv2.at[c])
        for c in range(CLIPS)
    ]
    sums = [
        [
            Exchange(
                "slab", slabs, terms.at[w, c], every.at[w, c], send1.at[w, c], recv1.at[w, c]
            )
            for c in range(CLIPS)
        ]
        for w in range(SWEEPS)
    ]

    def queries(w, c):
        own_queries(w, own[w][c], square, at_ref, bq_ref, qs.at[c])

    def finish(w, c):
        first = STEPS_DEV * lax.axis_index("slab")
        if w:
            first = first + slides_ref[0]
        levels = [plan_ref[first + a].astype(f32) for a in range(STEPS_DEV + 1)]
        sizes = [(levels[a + 1] - levels[a]) / 1000.0 for a in range(STEPS_DEV)]
        velocity_terms(
            w, sizes, own[w].at[c], zs.at[c], mv_ref, w_o, w_in, w_out_t, terms.at[w, c]
        )

    def send(w, c):
        sums[w][c].start()

    def slide(w, c):
        sums[w][c].wait()
        return picard(slides_ref[w], moved[c], every.at[w, c])

    def advance(c):
        state, moved[c] = slide(0, c)
        own1[c] = (anchor[c] + state).astype(bf16)
        gathers[c].start()

    def keys0(c):
        scales = [(bk_ref[s], rho.at[c, s]) for s in range(STEPS_DEV)]
        keys_of(xs.at[c], square, kf0.at[c], scales)

    def keys1(c, s):
        scales = [(bk_ref[STEPS_DEV + s], rho.at[c, s])]
        keys_of(xs.at[s], square, kf1.at[c, s], scales)

    def receive(c):
        gathers[c].wait()
        halves(all1.at[c], xs)
        keys1(c, 0)

    blocks = []
    for w in range(SWEEPS):
        for c in range(CLIPS):
            for s in range(STEPS_DEV):
                for part in range(per):
                    slot = len(blocks) % 2
                    blocks.append(
                        dict(
                            q=qs.at[c, s, part], kf=kf1.at[c, s] if w else kf0.at[c],
                            rho=rho.at[c, s], part=part, sc=(sc0, sc1)[slot], top=(top0, top1)[slot],
                            pr=(pr0, pr1)[slot], zs=zs.at[c, s],
                        )
                    )
    one = STEPS_DEV * per
    turn = CLIPS * one

    def stage(n, low, high):
        def pick(k):
            return blocks[k] if low <= k < high else None

        stages(pick(n), pick(n - 1), pick(n - 2), tokens)

    for c in range(CLIPS):
        queries(0, c)
    loads[6].wait()
    project(lhs, wv, m_ref, 2)
    for t in range(STEPS_DEV):
        fold_values(t, m_ref, mv_ref)
    loads[7].wait()
    loads[8].wait()
    gather0.wait()
    halves(all0, xs)
    keys0(0)
    for n in range(turn + 2):
        stage(n, 0, turn)
        if n == 0:
            keys0(1)
        if n == one + 1:
            finish(0, 0)
            send(0, 0)
        if n == turn:
            advance(0)
    finish(0, 1)
    send(0, 1)

    for t in range(STEPS_DEV, COMBOS):
        fold_scores(t, m_ref, gain, at_ref, bk_ref, bq_ref)
        fold_values(t, m_ref, mv_ref)

    queries(1, 0)
    advance(1)
    receive(0)
    for n in range(turn, 2 * turn + 2):
        if n == turn + one:
            queries(1, 1)
            receive(1)
        stage(n, turn, 2 * turn)
        if n in (turn, turn + one):
            keys1((n - turn) // one, 1)
        if n == turn + one + 1:
            finish(1, 0)
        if n == turn + one + 2:
            send(1, 0)
    finish(1, 1)
    send(1, 1)
    for c in range(CLIPS):
        state, last = slide(1, c)
        for s in range(STEPS_DEV):
            moved_ref[s, c] = state[:, OWN * s : OWN * (s + 1)]
        moved_ref[STEPS_DEV, c] = last[:, :OWN]


def add_kernel(noise_ref, moved_ref, states_ref, anchor_ref):
    for s in range(STEPS_DEV):
        states_ref[s] = noise_ref[...] + moved_ref[s]
    anchor_ref[...] = noise_ref[...] + moved_ref[STEPS_DEV]


def on_device(noise, plan, slides, w_in, w_mod, w_qkv, qk_gain, w_o, w_out):
    slabs, count = lax.axis_size("slab"), lax.axis_size("seq")
    tokens = count * OWN
    half = FREQ // 2
    freq = np.exp(-math.log(10000.0) * np.arange(half) / half).astype(np.float32)[None]
    smem = pl.BlockSpec(memory_space=pltpu.SMEM)
    vmem = pl.BlockSpec(memory_space=pltpu.VMEM)
    far = pl.BlockSpec(memory_space=pl.ANY)
    block = (PATCH, LANES)

    def sems(*shape):
        return [pltpu.SemaphoreType.DMA(shape), pltpu.SemaphoreType.DMA(shape)]

    moved = pl.pallas_call(
        window_kernel,
        in_specs=[smem, smem, vmem] + [far] * 7,
        out_specs=vmem,
        out_shape=jax.ShapeDtypeStruct((STEPS_DEV + 1, CLIPS, PATCH, OWN), f32),
        scratch_shapes=[
            pltpu.VMEM((CLIPS, PATCH, OWN), f32),
            pltpu.VMEM((PATCH, WIDTH), bf16),
            pltpu.VMEM((FREQ, 2 * WIDTH), bf16),
            pltpu.VMEM((WIDTH, WIDTH), bf16),
            pltpu.VMEM((WIDTH, WIDTH), bf16),
            pltpu.VMEM((WIDTH, WIDTH), bf16),
            pltpu.VMEM((2, WIDTH), f32),
            pltpu.VMEM((WIDTH, WIDTH), bf16),
            pltpu.VMEM((PATCH, WIDTH), bf16),
            pltpu.SemaphoreType.DMA((9,)),
            pltpu.VMEM((2 * COMBOS * FE, WIDTH), bf16),
            pltpu.VMEM((COMBOS, FE, 3 * WIDTH), f32),
            pltpu.VMEM((3 * PATCH, PATCH), bf16),
            pltpu.VMEM((COMBOS, HEADS * LANES, LANES), bf16),
            pltpu.VMEM((COMBOS, HEADS * TERMS, LANES), bf16),
            pltpu.VMEM((COMBOS, HEADS * TERMS, LANES), bf16),
            pltpu.VMEM((COMBOS, 2, HEADS * 16, WIDE), bf16),
            pltpu.VMEM((CLIPS,) + block, f32),
            pltpu.VMEM((CLIPS,) + block, f32),
            pltpu.VMEM(block, bf16),
            pltpu.VMEM((CLIPS,) + block, bf16),
            pltpu.VMEM((CLIPS,) + block, bf16),
            pltpu.VMEM((count,) + block, bf16),
            pltpu.VMEM((CLIPS, count) + block, bf16),
            pltpu.VMEM((SWEEPS, CLIPS) + block, f32),
            pltpu.VMEM((SWEEPS, CLIPS, slabs) + block, f32),
            *sems(1), *sems(SWEEPS, CLIPS), *sems(CLIPS),
            pltpu.VMEM((2, PATCH, tokens), f32),
            pltpu.VMEM((CLIPS, LANES, tokens), bf16),
            pltpu.VMEM((CLIPS, STEPS_DEV, LANES, tokens), bf16),
            pltpu.VMEM((CLIPS, STEPS_DEV, GROUPS, 8, tokens), f32),
            pltpu.VMEM((CLIPS, STEPS_DEV, HEADS // HB, ROWS, LANES), bf16),
            pltpu.VMEM((ROWS, tokens), f32),
            pltpu.VMEM((ROWS, tokens), f32),
            pltpu.VMEM((ROWS, tokens), bf16),
            pltpu.VMEM((ROWS, tokens), bf16),
            pltpu.VMEM((ROWS, LANES), f32),
            pltpu.VMEM((ROWS, LANES), f32),
            pltpu.VMEM((CLIPS, STEPS_DEV, GROUPS, OWN, LANES), bf16),
        ],
        compiler_params=pltpu.CompilerParams(
            collective_id=1, has_side_effects=True, vmem_limit_bytes=56 << 20
        ),
    )(plan, slides, freq, noise, w_in, w_mod, w_qkv, qk_gain, w_o, w_out.T)
    return pl.pallas_call(
        add_kernel,
        in_specs=[vmem, vmem],
        out_specs=[vmem, vmem],
        out_shape=[
            jax.ShapeDtypeStruct((STEPS_DEV, CLIPS, PATCH, OWN), f32),
            jax.ShapeDtypeStruct((CLIPS, PATCH, OWN), f32),
        ],
    )(noise, moved)


def solution(mesh):
    return jax.shard_map(
        on_device,
        mesh=mesh,
        in_specs=(P(None, None, "seq"), P(), P(), P(), P(), P(), P(), P(), P()),
        out_specs=(P("slab", None, None, "seq"), P(None, None, "seq")),
        check_vma=False,
    )
```
